256 devices in a mesh: ctx: 16 (over z, x_lo), head: 8 (over y, x_hi), rep: 2 (over core).
Axes of the slice: x: 4 (x_hi: 2, x_lo: 2; x = x_hi * 2 + x_lo), y: 4, z: 8, core: 2. Of those that a mesh axis runs over, the one named last changes fastest.
Arguments:
- queries: bfloat16 [2, 4096, 4096], P('rep', 'ctx', 'head'), may hold values from -1.1953125 to 1.1953125
- key_vecs: bfloat16 [2, 4096, 4096], P('rep', 'ctx', 'head'), may hold values from -1.1953125 to 1.1953125
- values: bfloat16 [2, 4096, 4096], P('rep', 'ctx', 'head'), may hold values from -6 to 6
- out_grad: bfloat16 [2, 4096, 4096], P('rep', 'ctx', 'head'), may hold values from -6 to 6
- out_weight: bfloat16 [4096, 4096], P('head', 'ctx'), may hold values from -0.09375 to 0.09375
- sign_bits: int32 [32, 3, 256], P('head'), may hold values from 0 to 1
Outputs:
- query_grad: bfloat16 [2, 4096, 4096], P('rep', 'ctx', 'head')
- key_grad: bfloat16 [2, 4096, 4096], P('rep', 'ctx', 'head')
- value_grad: bfloat16 [2, 4096, 4096], P('rep', 'ctx', 'head')
- out_weight_grad: bfloat16 [4096, 4096], P('head', 'ctx')
The draws below stay inside these ranges and needn't reach their ends.
Inputs may be any that keep to these rules, and one draw needn't show every extreme that they name: `sign_bits`: each entry is a bit; the sign it gives is 2 bit - 1.
All inputs are finite; a program needn't handle non-finite values.
Results may differ from the reference program's by a relative error of at most 0.0095.
Values may be sent and summed in bfloat16 or wider, within the bound.
A program may use at most 128 MiB of HBM per device.

```python
import math
import jax
import jax.numpy as jnp
from jax import lax

D = 4096
HEADS = 32
DH = 128
M = 256
GROUP = 256
SEQ = 4096
BATCH = 2


def set_ends(drawn, rng, smallest, largest):
    longest = drawn.shape.index(max(drawn.shape))
    spots = []
    for shift in (0, 1):
        where = [jax.random.randint(jax.random.fold_in(rng, axis), (), 0, length) for axis, length in enumerate(drawn.shape)]
        where[longest] = (where[longest] + shift) % drawn.shape[longest]
        spots.append(tuple(where))
    return drawn.at[spots[0]].set(smallest).at[spots[1]].set(largest)


def with_spikes(values, stream_key, source, target, parts, factor):
    def block_of(axis_at):
        return (jnp.arange(values.shape[axis_at]) // (values.shape[axis_at] // parts)).reshape((-1,) + (1,) * (values.ndim - 1 - axis_at))

    near = jax.random.permutation(stream_key, parts)[block_of(target)]
    second = (block_of(target) + parts // 2) % parts
    return jnp.where((block_of(source) == near) | (block_of(source) == second), factor * values, values)


def shard_levels(own_key, dims, pieces, least, top_value):
    factor_of = 1.0
    for dim, shards_of in pieces:
        steps = jax.random.uniform(jax.random.fold_in(jax.random.fold_in(own_key, 6), dim), (shards_of,), jnp.float32, least / len(pieces), top_value / len(pieces))
        factor_of = factor_of * jnp.repeat(jnp.exp(steps), dims[dim] // shards_of).reshape((-1,) + (1,) * (len(dims) - 1 - dim))
    return factor_of


def normal_values(key, dims, spread, most, pieces=(), kind=jnp.bfloat16):
    result = jax.random.normal(key, dims, jnp.float32) * spread
    if len(pieces) > 0:
        result = shard_levels(key, dims, pieces, -0.22, 0.18) * result
    return jnp.clip(result, min=-most, max=most).astype(kind)


def gaussian_with(rng, shape, scale, reach, pieces, heavy, kind=jnp.bfloat16):
    entries = scale * jax.random.normal(rng, shape, jnp.float32)
    if pieces:
        entries = entries * shard_levels(rng, shape, pieces, -0.22, 0.18)
    return jnp.clip(with_spikes(entries, jax.random.fold_in(rng, 3), *heavy), -reach, reach).astype(kind)


def setup_inputs(seed: int = 0) -> dict:
    keys = jax.random.split(jax.random.key(seed), 7)
    queries = normal_values(keys[0], (BATCH, SEQ, HEADS * DH), 0.4, 1.1953125, ((0, 2), (1, 16), (2, 8)))
    key_vecs = normal_values(keys[1], (BATCH, SEQ, HEADS * DH), 0.4, 1.1953125, ((0, 2), (1, 16), (2, 8)))
    values = normal_values(keys[2], (BATCH, SEQ, HEADS * DH), 1.0, 6.0, ((0, 2), (1, 16), (2, 8)))
    out_grad = gaussian_with(keys[3], (BATCH, SEQ, D), 1.0, 6.0, ((0, 2), (1, 16), (2, 8)), (1, 2, 16, 2.0))
    out_weight = normal_values(keys[4], (HEADS * DH, D), (HEADS * DH) ** -0.5, 0.09375, ((0, 8), (1, 16)))
    sign_bits = set_ends(jax.random.randint(keys[5], (HEADS, 3, M), 0, 2), jax.random.fold_in(keys[5], 1), 0, 1).astype(jnp.int32)
    return {"queries": queries, "key_vecs": key_vecs, "values": values, "out_grad": out_grad, "out_weight": out_weight, "sign_bits": sign_bits}


TOP_PRECISION = lax.Precision.HIGHEST

def hadamard_table(order):
    row_index = jnp.arange(order, dtype=jnp.int32)[:, None]
    col_index = jnp.arange(order, dtype=jnp.int32)[None, :]
    common = jnp.bitwise_and(row_index, col_index)
    parity = jnp.zeros((order, order), jnp.int32)
    for place in range(order.bit_length()):
        parity = parity + jnp.bitwise_and(jnp.right_shift(common, place), 1)
    return (1 - 2 * (parity % 2)).astype(jnp.float32)

def sign_matrix(bits):
    signs = 2.0 * bits.astype(jnp.float32) - 1.0
    hadam = hadamard_table(DH)
    blocks = []
    for block in range(M // DH):
        piece = signs[:, block * DH:(block + 1) * DH]
        mixing_matrix = hadam * piece[2][None, :]
        mixing_matrix = jnp.dot(hadam, piece[1][:, None] * mixing_matrix, precision=TOP_PRECISION)
        mixing_matrix = jnp.dot(hadam, piece[0][:, None] * mixing_matrix, precision=TOP_PRECISION)
        blocks.append(mixing_matrix / DH)
    return jnp.concatenate(blocks, axis=0)

def feature_map(rows, mixing_matrix):
    rescaled_rows = rows.astype(jnp.float32) * DH ** (-0.25)
    random_projection = jnp.dot(rescaled_rows, mixing_matrix.T, precision=TOP_PRECISION)
    feats = jnp.exp(random_projection - 0.5 * lax.optimization_barrier(jnp.sum(rescaled_rows * rescaled_rows, axis=-1, keepdims=True))) / math.sqrt(M)
    return (rescaled_rows, feats)

def feature_back(grad_feat, rescaled_rows, feats, mixing_matrix):
    weighted_rows = grad_feat * feats
    backward_fn = jnp.dot(weighted_rows, mixing_matrix, precision=TOP_PRECISION) - rescaled_rows * lax.optimization_barrier(jnp.sum(weighted_rows, axis=-1, keepdims=True))
    return (DH ** (-0.25) * backward_fn).astype(jnp.bfloat16)

def fmix(form, left, right):
    return jnp.einsum(form, left.astype(jnp.float32), right.astype(jnp.float32), precision=TOP_PRECISION)

def one_head(items):
    qrows, krows, vrows, grad_o, mixing_matrix = items
    nchunk = SEQ // GROUP
    q_scaled, q_feat = feature_map(qrows, mixing_matrix)
    k_scaled, k_feat = feature_map(krows, mixing_matrix)
    qf = q_feat.astype(jnp.bfloat16).reshape(nchunk, GROUP, M)
    kf = k_feat.astype(jnp.bfloat16).reshape(nchunk, GROUP, M)
    vals = vrows.reshape(nchunk, GROUP, DH)
    causal = jnp.arange(GROUP)[:, None] >= jnp.arange(GROUP)[None, :]
    causal_masked = jnp.where(causal[None], fmix('ntm,nsm->nts', qf, kf), 0.0)
    masked_b = causal_masked.astype(jnp.bfloat16)
    group_kv = fmix('nsm,nsd->nmd', kf, vals)
    group_kz = lax.optimization_barrier(jnp.sum(kf.astype(jnp.float32), axis=1))
    kv_prev = jnp.cumsum(group_kv, axis=0) - group_kv
    kz_prev = jnp.cumsum(group_kz, axis=0) - group_kz
    kv_prev_b = kv_prev.astype(jnp.bfloat16)
    numer = fmix('nts,nsd->ntd', masked_b, vals) + fmix('ntm,nmd->ntd', qf, kv_prev_b)
    denom = lax.optimization_barrier(jnp.sum(causal_masked, axis=-1)) + fmix('ntm,nm->nt', qf, kz_prev)
    attn = numer / denom[..., None]
    attn_b = attn.astype(jnp.bfloat16)
    grad_o = grad_o.reshape(nchunk, GROUP, DH)
    grad_num_b = (grad_o / denom[..., None]).astype(jnp.bfloat16)
    grad_den = -lax.optimization_barrier(jnp.sum(grad_o * attn, axis=-1)) / denom
    group_rq = fmix('ntm,ntd->nmd', qf, grad_num_b)
    group_rz = fmix('ntm,nt->nm', qf, grad_den)
    rq_next = lax.optimization_barrier(jnp.sum(group_rq, axis=0))[None] - jnp.cumsum(group_rq, axis=0)
    rz_next = lax.optimization_barrier(jnp.sum(group_rz, axis=0))[None] - jnp.cumsum(group_rz, axis=0)
    rq_next_b = rq_next.astype(jnp.bfloat16)
    mixed = jnp.where(causal[None], fmix('ntd,nsd->nts', grad_num_b, vals) + grad_den[:, :, None], 0.0).astype(jnp.bfloat16)
    grad_qf = fmix('nts,nsm->ntm', mixed, kf) + fmix('ntd,nmd->ntm', grad_num_b, kv_prev_b) + grad_den[..., None] * kz_prev[:, None, :]
    grad_kf = fmix('nts,ntm->nsm', mixed, qf) + fmix('nsd,nmd->nsm', vals, rq_next_b) + rz_next[:, None, :]
    grad_v = fmix('nts,ntd->nsd', masked_b, grad_num_b) + fmix('nsm,nmd->nsd', kf, rq_next_b)
    query_part = feature_back(grad_qf.reshape(SEQ, M), q_scaled, q_feat, mixing_matrix)
    key_part = feature_back(grad_kf.reshape(SEQ, M), k_scaled, k_feat, mixing_matrix)
    return (query_part, key_part, grad_v.reshape(SEQ, DH).astype(jnp.bfloat16), attn_b.reshape(SEQ, DH))

def split_heads(array):
    return array.reshape(BATCH, SEQ, HEADS, DH).transpose(0, 2, 1, 3).reshape(BATCH * HEADS, SEQ, DH)

def join_heads(array):
    return array.reshape(BATCH, HEADS, SEQ, DH).transpose(0, 2, 1, 3).reshape(BATCH, SEQ, HEADS * DH)

def reference(queries, key_vecs, values, out_grad, out_weight, sign_bits):
    mixing_matrices = jax.vmap(sign_matrix)(sign_bits)
    flat_grad = out_grad.reshape(BATCH * SEQ, D)
    head_grad = jnp.dot(flat_grad, out_weight.T, preferred_element_type=jnp.float32)
    head_grad = head_grad.reshape(BATCH, SEQ, HEADS * DH)
    items = (split_heads(queries), split_heads(key_vecs), split_heads(values), split_heads(head_grad), jnp.tile(mixing_matrices, (BATCH, 1, 1)))
    query_grad, key_grad, value_grad, attn_b = lax.map(one_head, items)
    attn_flat = join_heads(attn_b).reshape(BATCH * SEQ, HEADS * DH)
    weight_grad = jnp.dot(attn_flat.T, flat_grad, preferred_element_type=jnp.float32).astype(jnp.bfloat16)
    return (join_heads(query_grad), join_heads(key_grad), join_heads(value_grad), weight_grad)
```

```python
import functools

import jax
import jax.numpy as jnp
from jax import lax
from jax.experimental import pallas as pl
from jax.experimental.pallas import tpu as pltpu
from jax.sharding import PartitionSpec as P

DH = 128
M = 256
T = 256
HL = 4
NZ = 8
NC = 16
SL = 80
C = DH ** (-0.25)
F32 = jnp.float32
BF16 = jnp.bfloat16
MESH = pl.DeviceIdType.MESH

AX = 0
AYP, AYM, AYP2, AYM2 = 4, 8, 12, 14
AC = 16
BZP, BZM, BC = 20, 24, 27
GX, AT, CP, CM, CC = 34, 35, 38, 42, 45
D1A, D1B, D2A, D2B = 46, 62, 78, 94
NSEM = 110


def dot_nn(a, b):
    return lax.dot_general(a, b, (((1,), (0,)), ((), ())), preferred_element_type=F32)


def dot_nt(a, b):
    return lax.dot_general(a, b, (((1,), (1,)), ((), ())), preferred_element_type=F32)


def dot_tn(a, b):
    return lax.dot_general(a, b, (((0,), (0,)), ((), ())), preferred_element_type=F32)


def hadamard():
    i = lax.broadcasted_iota(jnp.int32, (DH, DH), 0)
    j = lax.broadcasted_iota(jnp.int32, (DH, DH), 1)
    x = i & j
    x = x ^ (x >> 4)
    x = x ^ (x >> 2)
    x = x ^ (x >> 1)
    return (1 - 2 * (x & 1)).astype(F32)


def head_cols(i):
    return pl.ds(pl.multiple_of(i * DH, DH), DH)


def kernel(q_ref, k_ref, v_ref, og_ref, ow_ref, sb_ref,
           qg_ref, kg_ref, vg_ref, wg_ref,
           ogg, owg, gacc, gsend, grecv,
           st, rv, po, pr, st2, rv2, po2, pr2,
           wc, pq, pk, qf, kf, ab, nv, rs, rd, attn, at, atg,
           gnb, gd, dk0, dv0, cps, cms, crp, crm,
           ssem, rsem):
    ctx = lax.axis_index("ctx")
    head = lax.axis_index("head")
    rep = lax.axis_index("rep")
    z, xl = ctx // 2, ctx % 2
    y, xh = head // 2, head % 2
    x = xh * 2 + xl
    sib = {"rep": 1 - rep}
    pair_ctx = z * 2 + 1 - xl
    pair = {"ctx": pair_ctx}
    pair_sib = {"ctx": pair_ctx, "rep": 1 - rep}
    yp = {"head": (head + 2) % 8}
    ym = {"head": (head + 6) % 8}
    zp = {"ctx": (ctx + 2) % NC}
    zm = {"ctx": (ctx + NC - 2) % NC}

    def xdev(k):
        xx = (x + k) % 4
        return {"ctx": z * 2 + xx % 2, "head": y * 2 + xx // 2}

    def rcopy(src, dst, n, dev):
        return pltpu.make_async_remote_copy(
            src_ref=src, dst_ref=dst, send_sem=ssem.at[n], recv_sem=rsem.at[n],
            device_id=dev, device_id_type=MESH)

    barrier = pltpu.get_barrier_semaphore()

    def greet(d, _):
        pl.semaphore_signal(barrier, inc=1, device_id={"ctx": (ctx + d) % NC}, device_id_type=MESH)
        return 0

    lax.fori_loop(1, NC, greet, 0)
    for dev in (sib, pair_sib, yp, ym):
        pl.semaphore_signal(barrier, inc=1, device_id=dev, device_id_type=MESH)
    for k in range(1, 4):
        xx = (x + k) % 4

        @pl.when(xx // 2 != xh)
        def _():
            pl.semaphore_signal(barrier, inc=1, device_id=xdev(k), device_id_type=MESH)

    hd = hadamard()
    hb = hd.astype(BF16)

    def mixing(i, _):
        bits = sb_ref[i].astype(F32) * 2.0 - 1.0
        for blk in range(2):
            s = bits[:, blk * DH:(blk + 1) * DH]
            inner = dot_nn((hd * s[1:2]).astype(BF16), hb).astype(BF16)
            w = dot_nn((hd * s[0:1]).astype(BF16), inner) * (s[2:3] * (1.0 / DH))
            hi = w.astype(BF16)
            lo = (w - hi.astype(F32)).astype(BF16)
            wc[i, blk * DH:(blk + 1) * DH, 0:DH] = hi
            wc[i, blk * DH:(blk + 1) * DH, DH:2 * DH] = lo
        return 0

    lax.fori_loop(0, HL, mixing, 0)

    pl.semaphore_wait(barrier, 21)

    def half(s):
        return og_ref.at[:, pl.ds(pl.multiple_of(s * 256, 256), 256)]

    my_b = head
    ax = []
    for k in range(1, 4):
        xx = (x + k) % 4
        c = rcopy(half(xx % 2), ogg.at[0, my_b, xl], AX + k, xdev(k))
        c.start()
        ax.append(c)

    rows_r = pl.ds(pl.multiple_of(rep * 256, 256), 256)

    bzp, bzm = [], []
    owg[z] = ow_ref[...]

    def z_send(s, up):
        blk = (z + NZ - s) % NZ if up else (z + s) % NZ
        ref = owg.at[blk, rows_r]
        c = rcopy(ref, ref, (BZP if up else BZM) + s, zp if up else zm)
        c.start()
        (bzp if up else bzm).append(c)

    z_send(0, True)
    z_send(0, False)

    def piece(yy, k):
        xx = (x + 4 - k) % 4
        return ogg.at[0, yy * 2 + xx // 2, xx % 2]

    sends = []
    ayp, aym = {}, {}

    def y_send(k):
        p = piece(y, k)
        ayp[k] = rcopy(p, p, AYP + k, yp)
        aym[k] = rcopy(p, p, AYM + k, ym)
        ayp[k].start()
        aym[k].start()

    ogg[0, my_b, xl] = og_ref[:, pl.ds(pl.multiple_of(xl * 256, 256), 256)]
    y_send(0)

    def features(x_ref, i):
        xb = x_ref[:, head_cols(i)]
        xf = xb.astype(F32)
        proj = dot_nt(jnp.concatenate([xb, xb], axis=1), wc[i]) * C
        norm = jnp.sum(xf * xf, axis=-1, keepdims=True) * (0.5 * C * C)
        return jnp.exp(proj - norm) * (1.0 / 16.0)

    def put_state(buf, i, s, zrow):
        zh = zrow.astype(BF16).astype(F32)
        zl = zrow - zh
        rowid = lax.broadcasted_iota(jnp.int32, (16, DH), 0)
        sb = s.astype(BF16)
        for t in range(4):
            g = slice((t // 2) * DH, (t // 2 + 1) * DH)
            buf[4 * i + t, 0:64, :] = sb[64 * t:64 * (t + 1)]
            buf[4 * i + t, 64:80, :] = jnp.where(
                rowid == 0, zh[:, g], jnp.where(rowid == 1, zl[:, g], 0.0)).astype(BF16)

    def get_state(buf, i):
        s = jnp.concatenate([buf[4 * i + t, 0:64, :] for t in range(4)], axis=0)
        za = buf[4 * i, 64:80, :].astype(F32)
        zb = buf[4 * i + 2, 64:80, :].astype(F32)
        zrow = jnp.concatenate([za[0:1] + za[1:2], zb[0:1] + zb[1:2]], axis=1)
        return s, zrow

    def k_phase(i, _):
        p = features(k_ref, i)
        pk[i] = p
        kb = p.astype(BF16)
        kf[i] = kb
        put_state(st, i, dot_tn(kb, v_ref[:, head_cols(i)]),
                  jnp.sum(kb.astype(F32), axis=0, keepdims=True))
        return 0

    lax.fori_loop(0, HL, k_phase, 0)

    def scan_copy(src, dst, n, d):
        to = (ctx + d) % NC
        return rcopy(src.at[to], dst.at[ctx], n + d, {"ctx": to})

    def scan_each(fn):
        lax.fori_loop(1, NC, lambda d, _: (fn(d), 0)[1], 0)

    def scan_send(src, dst, n):
        scan_each(lambda d: scan_copy(src, dst, n, d).start())

    def scan_recv(src, dst, n):
        scan_each(lambda d: scan_copy(src, dst, n, d).wait_recv())

    def scan_sent(src, dst, n):
        scan_each(lambda d: scan_copy(src, dst, n, d).wait_send())

    def running(rbuf, obuf, backward):
        rowid = lax.broadcasted_iota(jnp.int32, (16, DH), 0)

        def step(n, carry):
            cs, cz = carry
            c = NC - 1 - n if backward else n
            ch = cz.astype(BF16).astype(F32)
            cl = cz - ch
            obuf[c, 0:64, :] = cs.astype(BF16)
            obuf[c, 64:80, :] = jnp.where(
                rowid == 0, ch, jnp.where(rowid == 1, cl, 0.0)).astype(BF16)
            zin = rbuf[c, 64:80, :].astype(F32)
            return cs + rbuf[c, 0:64, :].astype(F32), cz + zin[0:1] + zin[1:2]

        lax.fori_loop(0, NC, step, (jnp.zeros((64, DH), F32), jnp.zeros((1, DH), F32)))

    scan_send(st, rv, D1A)

    for k in range(1, 4):
        ax[k - 1].wait_recv()
        y_send(k)

    bc = []

    def b_recv(s, up):
        (bzp if up else bzm)[s].wait_recv()
        blk = (z + NZ - 1 - s) % NZ if up else (z + 1 + s) % NZ
        ref = owg.at[blk, rows_r]
        if s + 1 < (4 if up else 3):
            z_send(s + 1, up)
        c = rcopy(ref, ref, BC + (s if up else 4 + s), sib)
        c.start()
        bc.append(c)

    ac = []

    def a_sib(n):
        yy = (y + n) % 4
        c = rcopy(ogg.at[0, pl.ds(yy * 2, 2)], ogg.at[1, pl.ds(yy * 2, 2)], AC + n, sib)
        c.start()
        ac.append(c)

    b_recv(0, True)
    b_recv(0, False)
    a_sib(0)

    tri = (lax.broadcasted_iota(jnp.int32, (T, T), 0)
           >= lax.broadcasted_iota(jnp.int32, (T, T), 1))

    def q_phase(i, _):
        p = features(q_ref, i)
        pq[i] = p
        qb = p.astype(BF16)
        qf[i] = qb
        am = jnp.where(tri, dot_nt(qb, kf[i]), 0.0)
        rs[i] = jnp.sum(am, axis=-1, keepdims=True)
        amb = am.astype(BF16)
        ab[i] = amb
        nv[i] = dot_nn(amb, v_ref[:, head_cols(i)])
        return 0

    lax.fori_loop(0, HL, q_phase, 0)

    b_recv(1, True)
    b_recv(1, False)

    scan_recv(st, rv, D1A)
    rv[ctx] = st[ctx]
    running(rv, po, False)
    pr[ctx] = po[ctx]
    scan_send(po, pr, D1B)

    b_recv(2, True)
    b_recv(2, False)

    ay2 = []
    for k in range(4):
        ayp[k].wait_recv()
        if k < 2:
            p = piece((y + 3) % 4, k)
            c = rcopy(p, p, AYP2 + k, yp)
            c.start()
            ay2.append(c)
        aym[k].wait_recv()
        if k >= 2:
            p = piece((y + 1) % 4, k)
            c = rcopy(p, p, AYM2 + k - 2, ym)
            c.start()
            ay2.append(c)
    b_recv(3, True)
    a_sib(3)
    a_sib(1)

    scan_recv(po, pr, D1B)

    def attn_phase(i, _):
        s, zrow = get_state(pr, i)
        qb = qf[i]
        den = rs[i] + jnp.sum(qb.astype(F32) * zrow, axis=-1, keepdims=True)
        r = 1.0 / den
        rd[i] = r
        a = (nv[i] + dot_nn(qb, s)) * r
        attn[i] = a
        at[i] = a.astype(BF16).T
        return 0

    lax.fori_loop(0, HL, attn_phase, 0)

    def at_half(n):
        return at.at[pl.ds(n * 2, 2)]

    atc = [rcopy(at_half(1 - rep), atg.at[1, xl], AT, sib),
           rcopy(at_half(rep), atg.at[0, xl], AT + 1, pair),
           rcopy(at_half(1 - rep), atg.at[1, xl], AT + 2, pair_sib)]
    for c in atc:
        c.start()
    atg[0, xl] = at[pl.ds(rep * 2, 2)]

    for c in bc:
        c.wait_recv()

    def go_group(n):
        yy = (y + n) % 4

        def tile(m, _):
            rows = pl.ds(pl.multiple_of(m % 2 * 128, 128), 128)
            acc = dot_nt(ogg[0, yy * 2, m // 2, rows, :], owg[yy * 2])
            acc += dot_nt(ogg[0, yy * 2 + 1, m // 2, rows, :], owg[yy * 2 + 1])
            if n == 0:
                gacc[m // 2, rows, :] = acc
            elif n == 2:
                total = gacc[m // 2, rows, :] + acc
                gacc[m // 2, rows, :] = total
                gsend[m // 2, rows, :] = total.astype(BF16)
            else:
                gacc[m // 2, rows, :] += acc
            return 0

        lax.fori_loop(0, 4, tile, 0)

    go_group(0)
    go_group(1)
    go_group(3)
    for c in ay2:
        c.wait_recv()
    a_sib(2)
    go_group(2)
    gx = rcopy(gsend.at[1 - xl], grecv, GX, pair)
    gx.start()

    for c in atc:
        c.wait_recv()
    for c in ac:
        c.wait_recv()

    def w_block(b):
        out = None
        for s in range(2):
            for t in range(2):
                a = jnp.concatenate([atg[s, t, 0], atg[s, t, 1]], axis=0)
                d = dot_nn(a, ogg[s, b, t])
                out = d if out is None else out + d
        return out

    cp, cm = [], []

    def c_up(s):
        val = w_block((z + 4 - s) % NZ)
        if s > 0:
            cp[s - 1].wait_recv()
            val += crp[s - 1].astype(F32)
        cps[s] = val.astype(BF16)
        c = rcopy(cps.at[s], crp.at[s], CP + s, zp)
        c.start()
        cp.append(c)

    def c_down(s):
        val = w_block((z + 5 + s) % NZ)
        if s > 0:
            cm[s - 1].wait_recv()
            val += crm[s - 1].astype(F32)
        cms[s] = val.astype(BF16)
        c = rcopy(cms.at[s], crm.at[s], CM + s, zm)
        c.start()
        cm.append(c)

    c_up(0)
    c_down(0)

    gx.wait_recv()

    def g_phase(i, _):
        cols = head_cols(i)
        go = gacc[xl, :, cols] + grecv[:, cols].astype(F32)
        r = rd[i]
        gb = (go * r).astype(BF16)
        gnb[i] = gb
        g = -jnp.sum(go * attn[i], axis=-1, keepdims=True) * r
        gd[i] = g
        qb = qf[i]
        put_state(st2, i, dot_tn(qb, gb), jnp.sum(qb.astype(F32) * g, axis=0, keepdims=True))
        return 0

    lax.fori_loop(0, HL, g_phase, 0)
    scan_send(st2, rv2, D2A)

    c_up(1)
    c_down(1)

    def back(i, x_ref, w, out_ref):
        hi = w.astype(BF16)
        lo = (w - hi.astype(F32)).astype(BF16)
        t = dot_nn(hi, wc[i]) + dot_nn(lo, wc[i])
        u = t[:, 0:DH] + t[:, DH:2 * DH]
        xf = x_ref[:, head_cols(i)].astype(F32) * C
        out_ref[:, head_cols(i)] = (C * (u - xf * jnp.sum(w, axis=-1, keepdims=True))).astype(BF16)

    def dq_phase(i, _):
        gb, g, kb, qb = gnb[i], gd[i], kf[i], qf[i]
        s, zrow = get_state(pr, i)
        bm = jnp.where(tri, dot_nt(gb, v_ref[:, head_cols(i)]) + g, 0.0).astype(BF16)
        dq = dot_nn(bm, kb) + dot_nt(gb, s) + g * zrow
        back(i, q_ref, dq * pq[i], qg_ref)
        dk0[i] = dot_tn(bm, qb)
        dv0[i] = dot_tn(ab[i], gb)
        return 0

    lax.fori_loop(0, 2, dq_phase, 0)

    scan_recv(st2, rv2, D2A)
    rv2[ctx] = st2[ctx]
    running(rv2, po2, True)
    pr2[ctx] = po2[ctx]
    scan_send(po2, pr2, D2B)

    c_up(2)
    c_down(2)
    lax.fori_loop(2, HL, dq_phase, 0)
    c_up(3)

    scan_recv(po2, pr2, D2B)

    def dk_phase(i, _):
        s, zrow = get_state(pr2, i)
        vb = v_ref[:, head_cols(i)]
        dk = dk0[i] + dot_nt(vb, s) + zrow
        back(i, k_ref, dk * pk[i], kg_ref)
        vg_ref[:, head_cols(i)] = (dv0[i] + dot_nn(kf[i], s)).astype(BF16)
        return 0

    lax.fori_loop(0, HL, dk_phase, 0)

    own = w_block(z)
    cp[3].wait_recv()
    cm[2].wait_recv()
    wg_ref[rows_r, :] = (own + crp[3].astype(F32) + crm[2].astype(F32)).astype(BF16)
    cc = rcopy(wg_ref.at[rows_r], wg_ref.at[rows_r], CC, sib)
    cc.start()

    for c in ax + bzp + bzm + list(ayp.values()) + list(aym.values()) + ay2 + bc + ac + atc + [gx] + cp + cm:
        c.wait_send()
    scan_sent(st, rv, D1A)
    scan_sent(po, pr, D1B)
    scan_sent(st2, rv2, D2A)
    scan_sent(po2, pr2, D2B)
    cc.wait()


def on_device(queries, key_vecs, values, out_grad, out_weight, sign_bits):
    flat = lambda a: a.reshape(T, HL * DH)
    vm = pl.BlockSpec(memory_space=pltpu.VMEM)
    state = pltpu.VMEM((NC, SL, DH), BF16)
    heads = lambda n, dt: pltpu.VMEM((HL, T, n), dt)
    blocks = lambda n: pltpu.VMEM((n, T, 256), BF16)
    qg, kg, vg, wg = pl.pallas_call(
        kernel,
        out_shape=[jax.ShapeDtypeStruct((T, HL * DH), BF16)] * 3
        + [jax.ShapeDtypeStruct((HL * DH, 256), BF16)],
        in_specs=[vm] * 6,
        out_specs=[vm] * 4,
        scratch_shapes=[
            pltpu.VMEM((2, 8, 2, T, 256), BF16),
            pltpu.VMEM((NZ, 512, 256), BF16),
            pltpu.VMEM((2, T, 512), F32),
            pltpu.VMEM((2, T, 512), BF16),
            pltpu.VMEM((T, 512), BF16),
            state, state, state, state, state, state, state, state,
            heads(256, BF16),
            heads(M, F32), heads(M, F32), heads(M, BF16), heads(M, BF16),
            heads(T, BF16), heads(DH, F32), heads(1, F32), heads(1, F32),
            heads(DH, F32),
            pltpu.VMEM((HL, DH, T), BF16),
            pltpu.VMEM((2, 2, 2, DH, T), BF16),
            heads(DH, BF16), heads(1, F32), heads(M, F32), heads(DH, F32),
            blocks(4), blocks(3), blocks(4), blocks(3),
            pltpu.SemaphoreType.DMA((NSEM,)),
            pltpu.SemaphoreType.DMA((NSEM,)),
        ],
        compiler_params=pltpu.CompilerParams(
            collective_id=0, has_side_effects=True, vmem_limit_bytes=48 * 1024 * 1024),
        cost_estimate=pl.CostEstimate(
            flops=5 * 10**9, bytes_accessed=4 * 10**6, transcendentals=5 * 10**5),
        name="performer_back",
    )(flat(queries), flat(key_vecs), flat(values), flat(out_grad), out_weight, sign_bits)
    shaped = lambda a: a.reshape(1, T, HL * DH)
    return shaped(qg), shaped(kg), shaped(vg), wg


def solution(mesh):
    tok = P("rep", "ctx", "head")
    return jax.shard_map(
        on_device, mesh=mesh,
        in_specs=(tok, tok, tok, tok, P("head", "ctx"), P("head", None, None)),
        out_specs=(tok, tok, tok, P("head", "ctx")),
        check_vma=False,
    )
```

```python
import functools

import jax
import jax.numpy as jnp
from jax import lax
from jax.experimental import pallas as pl
from jax.experimental.pallas import tpu as pltpu
from jax.sharding import PartitionSpec as P

DH = 128
M = 256
T = 256
HL = 4
NZ = 8
NC = 16
SR = 32
C = DH ** (-0.25)
F32 = jnp.float32
BF16 = jnp.bfloat16
MESH = pl.DeviceIdType.MESH

AX = 0
AYP, AYM, AYP2, AYM2 = 4, 8, 12, 14
AC = 16
BZP, BZM, BC = 20, 24, 27
GX, ATS, ATP = 34, 35, 36
CP, CM, CC = 38, 46, 52
D1A, D1B, D2A, D2B = 54, 56, 58, 60
ZB, RB = 62, 78
NSEM = 94


def dot_nn(a, b):
    return lax.dot_general(a, b, (((1,), (0,)), ((), ())), preferred_element_type=F32)


def dot_nt(a, b):
    return lax.dot_general(a, b, (((1,), (1,)), ((), ())), preferred_element_type=F32)


def dot_tn(a, b):
    return lax.dot_general(a, b, (((0,), (0,)), ((), ())), preferred_element_type=F32)


def hadamard():
    i = lax.broadcasted_iota(jnp.int32, (DH, DH), 0)
    j = lax.broadcasted_iota(jnp.int32, (DH, DH), 1)
    x = i & j
    x = x ^ (x >> 4)
    x = x ^ (x >> 2)
    x = x ^ (x >> 1)
    return (1 - 2 * (x & 1)).astype(F32)


def head_cols(i):
    return pl.ds(pl.multiple_of(i * DH, DH), DH)


def kernel(q_hbm, k_hbm, v_hbm, og_hbm, ow_hbm, sb_hbm,
           qg_ref, kg_ref, vg_ref, wg_ref,
           q_ref, k_ref, v_ref, sb_ref,
           ogg, owg, gacc, gsend, grecv,
           st, rv, po, pr, st2, rv2, po2, pr2, zs, zr, rs2, rr2, zpre,
           wc, pq, pk, qf, kf, ab, nv, rs, rd, attn, at, atg,
           gnb, gd, dk0, dv0, cps, cms, crp, crm,
           ssem, rsem, lsem):
    ctx = lax.axis_index("ctx")
    head = lax.axis_index("head")
    rep = lax.axis_index("rep")
    z, xl = ctx // 2, ctx % 2
    y, xh = head // 2, head % 2
    x = xh * 2 + xl
    sib = {"rep": 1 - rep}
    pair_ctx = z * 2 + 1 - xl
    pair = {"ctx": pair_ctx}
    pair_sib = {"ctx": pair_ctx, "rep": 1 - rep}
    yp = {"head": (head + 2) % 8}
    ym = {"head": (head + 6) % 8}
    zp = {"ctx": (ctx + 2) % NC}
    zm = {"ctx": (ctx + NC - 2) % NC}

    def xdev(k):
        xx = (x + k) % 4
        return {"ctx": z * 2 + xx % 2, "head": y * 2 + xx // 2}

    def rcopy(src, dst, n, dev):
        return pltpu.make_async_remote_copy(
            src_ref=src, dst_ref=dst, send_sem=ssem.at[n], recv_sem=rsem.at[n],
            device_id=dev, device_id_type=MESH)

    barrier = pltpu.get_barrier_semaphore()

    def greet(d, _):
        pl.semaphore_signal(barrier, inc=1, device_id={"ctx": (ctx + d) % NC}, device_id_type=MESH)
        return 0

    lax.fori_loop(1, NC, greet, 0)
    for dev in (sib, pair_sib, yp, ym):
        pl.semaphore_signal(barrier, inc=1, device_id=dev, device_id_type=MESH)
    for k in range(1, 4):
        xx = (x + k) % 4

        @pl.when(xx // 2 != xh)
        def _():
            pl.semaphore_signal(barrier, inc=1, device_id=xdev(k), device_id_type=MESH)

    def half(s):
        return og_hbm.at[:, pl.ds(pl.multiple_of(s * 256, 256), 256)]

    my_b = head
    rows_r = pl.ds(pl.multiple_of(rep * 256, 256), 256)
    local = [pltpu.make_async_copy(a, b, lsem.at[n]) for n, (a, b) in enumerate((
        (sb_hbm, sb_ref), (k_hbm, k_ref), (v_hbm, v_ref), (q_hbm, q_ref),
        (half(xl), ogg.at[0, my_b, xl]), (ow_hbm, owg.at[z])))]
    for c in local:
        c.start()

    hd = hadamard()
    hb = hd.astype(BF16)

    def mixing(i, _):
        bits = sb_ref[i].astype(F32) * 2.0 - 1.0
        for blk in range(2):
            s = bits[:, blk * DH:(blk + 1) * DH]
            inner = dot_nn((hd * s[1:2]).astype(BF16), hb).astype(BF16)
            w = dot_nn((hd * s[0:1]).astype(BF16), inner) * (s[2:3] * (1.0 / DH))
            hi = w.astype(BF16)
            lo = (w - hi.astype(F32)).astype(BF16)
            wc[i, blk * DH:(blk + 1) * DH, 0:DH] = hi
            wc[i, blk * DH:(blk + 1) * DH, DH:2 * DH] = lo
        return 0

    local[0].wait()
    lax.fori_loop(0, HL, mixing, 0)

    def features(x_ref, i):
        xb = x_ref[:, head_cols(i)]
        xf = xb.astype(F32)
        proj = dot_nt(jnp.concatenate([xb, xb], axis=1), wc[i]) * C
        norm = jnp.sum(xf * xf, axis=-1, keepdims=True) * (0.5 * C * C)
        return jnp.exp(proj - norm) * (1.0 / 16.0)

    def put_state(buf, i, s):
        sb = s.astype(BF16)
        for t in range(8):
            buf[i // 2, i % 2 * 8 + t] = sb[SR * t:SR * (t + 1)]

    def get_state(buf, i):
        return jnp.concatenate(
            [buf[i // 2, (ctx + NC - (i % 2 * 8 + t)) % NC] for t in range(8)], axis=0)

    def put_row(buf, i, row):
        buf[2 * i:2 * i + 1, :] = row[:, 0:DH]
        buf[2 * i + 1:2 * i + 2, :] = row[:, DH:2 * DH]

    def get_row(value, i):
        return jnp.concatenate([value[2 * i:2 * i + 1], value[2 * i + 1:2 * i + 2]], axis=1)

    local[1].wait()
    local[2].wait()
    for i in range(HL):
        p = features(k_ref, i)
        pk[i] = p
        kb = p.astype(BF16)
        kf[i] = kb
        put_state(st, i, dot_tn(kb, v_ref[:, head_cols(i)]))
        put_row(zs, i, jnp.sum(kb.astype(F32), axis=0, keepdims=True))

    def scan_send(src, dst, n, h):
        def go(d, _):
            to = (ctx + d) % NC
            rcopy(src.at[h, to], dst.at[h, d], n + h, {"ctx": to}).start()
            return 0

        lax.fori_loop(1, NC, go, 0)

    def scan_all(src, dst, n, h):
        rest = pl.ds(1, NC - 1)
        return rcopy(src.at[h, rest], dst.at[h, rest], n + h, pair)

    def running(rbuf, obuf, h, backward):
        def step(n, cs):
            c = NC - 1 - n if backward else n
            obuf[h, c] = cs.astype(BF16)
            return cs + rbuf[h, (ctx + NC - c) % NC].astype(F32)

        lax.fori_loop(0, NC, step, jnp.zeros((SR, DH), F32))

    def row_copy(src, dst, n, d, sign):
        return rcopy(src, dst.at[d], n + d, {"ctx": (ctx + sign * d + NC) % NC})

    def each(count, fn):
        lax.fori_loop(1, count + 1, lambda d, _: (fn(d), 0)[1], 0)

    pl.semaphore_wait(barrier, 21)

    later, earlier = NC - 1 - ctx, ctx
    each(later, lambda d: row_copy(zs, zr, ZB, d, 1).start())
    scan_send(st, rv, D1A, 0)

    ax = {}
    for k in (1, 3, 2):
        xx = (x + k) % 4
        ax[k] = rcopy(half(xx % 2), ogg.at[0, my_b, xl], AX + k, xdev(k))
        ax[k].start()

    def piece(yy, k):
        xx = (x + 4 - k) % 4
        return ogg.at[0, yy * 2 + xx // 2, xx % 2]

    ayp, aym, ay2 = {}, {}, {}

    def y_send(k):
        p = piece(y, k)
        src = half(xl) if k == 0 else p
        ayp[k] = rcopy(src, p, AYP + k, yp)
        aym[k] = rcopy(src, p, AYM + k, ym)
        ayp[k].start()
        aym[k].start()

    def y_relay(k):
        up = k < 2
        (ayp if up else aym)[k].wait_recv()
        p = piece((y + 3) % 4 if up else (y + 1) % 4, k)
        ay2[k] = rcopy(p, p, AYP2 + k if up else AYM2 + k - 2, yp if up else ym)
        ay2[k].start()

    y_send(0)

    bzp, bzm, bc = [], [], []

    def z_send(s, up):
        blk = (z + NZ - s) % NZ if up else (z + s) % NZ
        ref = owg.at[blk, rows_r]
        c = rcopy(ow_hbm.at[rows_r] if s == 0 else ref, ref,
                  (BZP if up else BZM) + s, zp if up else zm)
        c.start()
        (bzp if up else bzm).append(c)

    def b_recv(s, up):
        (bzp if up else bzm)[s].wait_recv()
        blk = (z + NZ - 1 - s) % NZ if up else (z + 1 + s) % NZ
        ref = owg.at[blk, rows_r]
        if s + 1 < (4 if up else 3):
            z_send(s + 1, up)
        c = rcopy(ref, ref, BC + (s if up else 4 + s), sib)
        c.start()
        bc.append(c)

    z_send(0, True)
    z_send(0, False)
    scan_send(st, rv, D1A, 1)

    tri = (lax.broadcasted_iota(jnp.int32, (T, T), 0)
           >= lax.broadcasted_iota(jnp.int32, (T, T), 1))

    def q_phase(i, _):
        p = features(q_ref, i)
        pq[i] = p
        qb = p.astype(BF16)
        qf[i] = qb
        am = jnp.where(tri, dot_nt(qb, kf[i]), 0.0)
        rs[i] = jnp.sum(am, axis=-1, keepdims=True)
        amb = am.astype(BF16)
        ab[i] = amb
        nv[i] = dot_nn(amb, v_ref[:, head_cols(i)])
        return 0

    local[3].wait()
    lax.fori_loop(0, 2, q_phase, 0)

    for k in (1, 3, 2):
        ax[k].wait_recv()
        y_send(k)
    b_recv(0, True)
    b_recv(0, False)

    lax.fori_loop(2, HL, q_phase, 0)

    each(earlier, lambda d: row_copy(zs, zr, ZB, d, 1).wait_recv())
    zsum = lax.fori_loop(1, ctx + 1, lambda d, a: a + zr[d], jnp.zeros((8, DH), F32))
    zpre[...] = zsum
    for i in range(HL):
        den = rs[i] + jnp.sum(qf[i].astype(F32) * get_row(zsum, i), axis=-1, keepdims=True)
        rd[i] = 1.0 / den

    def scan_turn(src, rbuf, obuf, dst, na, nb, h, backward):
        scan_all(src, rbuf, na, h).wait_recv()
        rbuf[h, 0] = src[h, ctx]
        running(rbuf, obuf, h, backward)
        dst[h, 0] = obuf[h, ctx]
        scan_send(obuf, dst, nb, h)

    ac = []

    def a_sib(n):
        yy = (y + n) % 4
        c = rcopy(ogg.at[0, pl.ds(yy * 2, 2)], ogg.at[1, pl.ds(yy * 2, 2)], AC + n, sib)
        c.start()
        ac.append(c)

    y_relay(1)
    y_relay(3)
    scan_turn(st, rv, po, pr, D1A, D1B, 0, False)
    b_recv(1, True)
    b_recv(1, False)
    y_relay(0)
    y_relay(2)
    scan_turn(st, rv, po, pr, D1A, D1B, 1, False)
    local[4].wait()
    local[5].wait()
    a_sib(0)
    b_recv(2, True)
    b_recv(2, False)
    b_recv(3, True)

    def go_part(mine):
        tok = xl if mine else 1 - xl

        def tile(m, _):
            rows = pl.ds(pl.multiple_of(m * 128, 128), 128)
            acc = dot_nt(ogg[0, 0, tok, rows, :], owg[0])
            for b in range(1, 8):
                acc += dot_nt(ogg[0, b, tok, rows, :], owg[b])
            if mine:
                gacc[rows, :] = acc
            else:
                gsend[rows, :] = acc.astype(BF16)
            return 0

        lax.fori_loop(0, 2, tile, 0)

    for c in bc:
        c.wait_recv()
    for k in (1, 3):
        (aym if k < 2 else ayp)[k].wait_recv()
        ay2[k].wait_recv()
    go_part(False)
    gx = rcopy(gsend, grecv, GX, pair)
    gx.start()

    atp = []
    ats = rcopy(at.at[pl.ds((1 - rep) * 2, 2)], atg.at[1, xl], ATS, sib)

    def attn_chunk(h):
        scan_all(po, pr, D1B, h).wait_recv()
        for i in (2 * h, 2 * h + 1):
            a = (nv[i] + dot_nn(qf[i], get_state(pr, i))) * rd[i]
            attn[i] = a
            at[i] = a.astype(BF16).T
        src = at.at[pl.ds(h * 2, 2)]
        c = rcopy(src, atg.at[(rep + h) % 2, xl], ATP + (rep + h) % 2, {"ctx": pair_ctx, "rep": h})
        c.start()
        atp.append(c)

        @pl.when(rep != h)
        def _():
            ats.start()

        @pl.when(rep == h)
        def _():
            atg[0, xl] = at[h * 2:h * 2 + 2]

    attn_chunk(0)
    attn_chunk(1)

    for k in (0, 2):
        (aym if k < 2 else ayp)[k].wait_recv()
        ay2[k].wait_recv()
    a_sib(1)
    a_sib(3)
    a_sib(2)
    go_part(True)

    gx.wait_recv()

    def g_chunk(h):
        for i in (2 * h, 2 * h + 1):
            cols = head_cols(i)
            go = gacc[:, cols] + grecv[:, cols].astype(F32)
            r = rd[i]
            gb = (go * r).astype(BF16)
            gnb[i] = gb
            g = -jnp.sum(go * attn[i], axis=-1, keepdims=True) * r
            gd[i] = g
            qb = qf[i]
            put_state(st2, i, dot_tn(qb, gb))
            put_row(rs2, i, jnp.sum(qb.astype(F32) * g, axis=0, keepdims=True))
        scan_send(st2, rv2, D2A, h)

    g_chunk(0)
    g_chunk(1)
    each(earlier, lambda d: row_copy(rs2, rr2, RB, d, -1).start())

    ats.wait_recv()
    for n in range(2):
        rcopy(atg.at[n, xl], atg.at[n, xl], ATP + n, pair).wait_recv()
    for c in ac:
        c.wait_recv()

    def w_block(b, ch):
        out = None
        for s in range(2):
            for t in range(2):
                d = dot_nn(atg[s, t, ch], ogg[s, b, t])
                out = d if out is None else out + d
        return out

    cp, cm = {}, {}

    def c_step(s, ch, up):
        sb, rb, cc = (cps, crp, cp) if up else (cms, crm, cm)
        val = w_block((z + 4 - s) % NZ if up else (z + 5 + s) % NZ, ch)
        if s > 0:
            cc[s - 1, ch].wait_recv()
            val += rb[s - 1, ch].astype(F32)
        sb[s, ch] = val.astype(BF16)
        c = rcopy(sb.at[s, ch], rb.at[s, ch], (CP if up else CM) + 2 * s + ch, zp if up else zm)
        c.start()
        cc[s, ch] = c

    def c_round(s):
        for ch in range(2):
            c_step(s, ch, True)
            if s < 3:
                c_step(s, ch, False)

    c_round(0)

    def back(i, x_ref, w, out_ref):
        hi = w.astype(BF16)
        lo = (w - hi.astype(F32)).astype(BF16)
        t = dot_nn(hi, wc[i]) + dot_nn(lo, wc[i])
        u = t[:, 0:DH] + t[:, DH:2 * DH]
        xf = x_ref[:, head_cols(i)].astype(F32) * C
        out_ref[:, head_cols(i)] = (C * (u - xf * jnp.sum(w, axis=-1, keepdims=True))).astype(BF16)

    def dq_phase(i):
        gb, g, kb, qb = gnb[i], gd[i], kf[i], qf[i]
        bm = jnp.where(tri, dot_nt(gb, v_ref[:, head_cols(i)]) + g, 0.0).astype(BF16)
        dq = dot_nn(bm, kb) + dot_nt(gb, get_state(pr, i)) + g * get_row(zpre[...], i)
        back(i, q_ref, dq * pq[i], qg_ref)
        dk0[i] = dot_tn(bm, qb)
        dv0[i] = dot_tn(ab[i], gb)

    dq_phase(0)
    c_round(1)
    dq_phase(1)

    scan_turn(st2, rv2, po2, pr2, D2A, D2B, 0, True)
    c_round(2)
    scan_turn(st2, rv2, po2, pr2, D2A, D2B, 1, True)
    dq_phase(2)
    c_round(3)
    dq_phase(3)

    each(later, lambda d: row_copy(rs2, rr2, RB, d, -1).wait_recv())
    rsum = lax.fori_loop(1, later + 1, lambda d, a: a + rr2[d], jnp.zeros((8, DH), F32))

    ccs = []

    def c_last(ch):
        own = w_block(z, ch)
        cp[3, ch].wait_recv()
        cm[2, ch].wait_recv()
        rows = pl.ds(pl.multiple_of(rep * 256 + ch * DH, DH), DH)
        wg_ref[rows, :] = (own + crp[3, ch].astype(F32) + crm[2, ch].astype(F32)).astype(BF16)
        c = rcopy(wg_ref.at[rows], wg_ref.at[rows], CC + ch, sib)
        c.start()
        ccs.append(c)

    def dk_chunk(h):
        scan_all(po2, pr2, D2B, h).wait_recv()
        for i in (2 * h, 2 * h + 1):
            s = get_state(pr2, i)
            vb = v_ref[:, head_cols(i)]
            dk = dk0[i] + dot_nt(vb, s) + get_row(rsum, i)
            back(i, k_ref, dk * pk[i], kg_ref)
            vg_ref[:, head_cols(i)] = (dv0[i] + dot_nn(kf[i], s)).astype(BF16)

    dk_chunk(0)
    c_last(0)
    c_last(1)
    dk_chunk(1)

    for group in (ax, ayp, aym, ay2, cp, cm):
        for c in group.values():
            c.wait_send()
    for c in bzp + bzm + bc + ac + atp + [ats, gx]:
        c.wait_send()
    for h in range(2):
        for src, dst, n in ((st, rv, D1A), (po, pr, D1B), (st2, rv2, D2A), (po2, pr2, D2B)):
            scan_all(src, dst, n, h).wait_send()
    each(later, lambda d: row_copy(zs, zr, ZB, d, 1).wait_send())
    each(earlier, lambda d: row_copy(rs2, rr2, RB, d, -1).wait_send())
    for c in ccs:
        c.wait()


def store(*refs):
    n = (len(refs) - 1) // 2
    copies = [pltpu.make_async_copy(refs[i], refs[n + i], refs[-1].at[i]) for i in range(n)]
    for c in copies:
        c.start()
    for c in copies:
        c.wait()


def on_device(queries, key_vecs, values, out_grad, out_weight, sign_bits):
    flat = lambda a: a.reshape(T, HL * DH)
    hbm = pl.BlockSpec(memory_space=pltpu.HBM)
    vm = pl.BlockSpec(memory_space=pltpu.VMEM)
    state = pltpu.VMEM((2, NC, SR, DH), BF16)
    row = pltpu.VMEM((8, DH), F32)
    rows = pltpu.VMEM((NC, 8, DH), F32)
    heads = lambda n, dt: pltpu.VMEM((HL, T, n), dt)
    blocks = lambda n: pltpu.VMEM((n, 2, DH, 256), BF16)
    act = pltpu.VMEM((T, HL * DH), BF16)
    shapes = [jax.ShapeDtypeStruct((T, HL * DH), BF16)] * 3 + [jax.ShapeDtypeStruct((HL * DH, 256), BF16)]
    grads = pl.pallas_call(
        kernel,
        out_shape=shapes,
        in_specs=[hbm] * 6,
        out_specs=[vm] * 4,
        scratch_shapes=[
            act, act, act, pltpu.VMEM((HL, 3, M), jnp.int32),
            pltpu.VMEM((2, 8, 2, T, 256), BF16),
            pltpu.VMEM((NZ, 512, 256), BF16),
            pltpu.VMEM((T, 512), F32),
            act, act,
            state, state, state, state, state, state, state, state,
            row, rows, row, rows, row,
            heads(256, BF16),
            heads(M, F32), heads(M, F32), heads(M, BF16), heads(M, BF16),
            heads(T, BF16), heads(DH, F32), heads(1, F32), heads(1, F32),
            heads(DH, F32),
            pltpu.VMEM((HL, DH, T), BF16),
            pltpu.VMEM((2, 2, 2, DH, T), BF16),
            heads(DH, BF16), heads(1, F32), heads(M, F32), heads(DH, F32),
            blocks(4), blocks(3), blocks(4), blocks(3),
            pltpu.SemaphoreType.DMA((NSEM,)),
            pltpu.SemaphoreType.DMA((NSEM,)),
            pltpu.SemaphoreType.DMA((6,)),
        ],
        compiler_params=pltpu.CompilerParams(
            collective_id=0, has_side_effects=True, vmem_limit_bytes=62 * 1024 * 1024),
        cost_estimate=pl.CostEstimate(
            flops=5 * 10**9, bytes_accessed=4 * 10**6, transcendentals=5 * 10**5),
        name="performer_back",
    )(flat(queries), flat(key_vecs), flat(values), flat(out_grad), out_weight, sign_bits)
    qg, kg, vg, wg = pl.pallas_call(
        store,
        out_shape=shapes,
        in_specs=[vm] * 4,
        out_specs=[hbm] * 4,
        scratch_shapes=[pltpu.SemaphoreType.DMA((4,))],
        name="store",
    )(*grads)
    shaped = lambda a: a.reshape(1, T, HL * DH)
    return shaped(qg), shaped(kg), shaped(vg), wg


def solution(mesh):
    tok = P("rep", "ctx", "head")
    return jax.shard_map(
        on_device, mesh=mesh,
        in_specs=(tok, tok, tok, tok, P("head", "ctx"), P("head", None, None)),
        out_specs=(tok, tok, tok, P("head", "ctx")),
        check_vma=False,
    )
```

```python
import functools

import jax
import jax.numpy as jnp
from jax import lax
from jax.experimental import pallas as pl
from jax.experimental.pallas import tpu as pltpu
from jax.sharding import PartitionSpec as P

DH = 128
M = 256
T = 256
HL = 4
NZ = 8
NC = 16
C = DH ** (-0.25)
F32 = jnp.float32
BF16 = jnp.bfloat16
MESH = pl.DeviceIdType.MESH

AX, AYP, AYM, AY2, AC = 0, 4, 8, 12, 16
BZP, BZM, BC = 32, 36, 39
GX, ATS, ATP = 46, 47, 48
CP, CM, CC = 50, 58, 64
D1, D2 = 65, 74
ZB, RB = 83, 98
NSEM = 114


def dot_nn(a, b):
    return lax.dot_general(a, b, (((1,), (0,)), ((), ())), preferred_element_type=F32)


def dot_nt(a, b):
    return lax.dot_general(a, b, (((1,), (1,)), ((), ())), preferred_element_type=F32)


def dot_tn(a, b):
    return lax.dot_general(a, b, (((0,), (0,)), ((), ())), preferred_element_type=F32)


def hadamard():
    i = lax.broadcasted_iota(jnp.int32, (DH, DH), 0)
    j = lax.broadcasted_iota(jnp.int32, (DH, DH), 1)
    x = i & j
    x = x ^ (x >> 4)
    x = x ^ (x >> 2)
    x = x ^ (x >> 1)
    return (1 - 2 * (x & 1)).astype(F32)


def head_cols(i):
    return pl.ds(pl.multiple_of(i * DH, DH), DH)


def kernel(q_hbm, k_hbm, v_hbm, og_hbm, ow_hbm, sb_hbm,
           qg_hbm, kg_hbm, vg_hbm, wg_hbm,
           q_ref, k_ref, v_ref, sb_ref, qg_ref, kg_ref, vg_ref, wg_ref,
           ogg, owg, gacc, gsend, grecv,
           st, l1, l2, tot, pf, pr, st2, l12, l22, tot2, pf2, pr2, run, zs, zr, rs2, rr2, zpre,
           wc, pq, pk, qf, kf, ab, nv, rs, rd, attn, at, atg,
           gnb, gd, dk0, dv0, cps, cms, crp, crm,
           ssem, rsem, lsem):
    ctx = lax.axis_index("ctx")
    head = lax.axis_index("head")
    rep = lax.axis_index("rep")
    z, xl = ctx // 2, ctx % 2
    y, xh = head // 2, head % 2
    x = xh * 2 + xl
    sib = {"rep": 1 - rep}
    pair_ctx = z * 2 + 1 - xl
    pair = {"ctx": pair_ctx}
    pair_sib = {"ctx": pair_ctx, "rep": 1 - rep}
    yp = {"head": (head + 2) % 8}
    ym = {"head": (head + 6) % 8}
    zp = {"ctx": (ctx + 2) % NC}
    zm = {"ctx": (ctx + NC - 2) % NC}

    def xdev(k):
        xx = (x + k) % 4
        return {"ctx": z * 2 + xx % 2, "head": y * 2 + xx // 2}

    def rcopy(src, dst, n, dev):
        return pltpu.make_async_remote_copy(
            src_ref=src, dst_ref=dst, send_sem=ssem.at[n], recv_sem=rsem.at[n],
            device_id=dev, device_id_type=MESH)

    barrier = pltpu.get_barrier_semaphore()

    def greet(d, _):
        pl.semaphore_signal(barrier, inc=1, device_id={"ctx": (ctx + d) % NC}, device_id_type=MESH)
        return 0

    lax.fori_loop(1, NC, greet, 0)
    for dev in (sib, pair_sib, yp, ym):
        pl.semaphore_signal(barrier, inc=1, device_id=dev, device_id_type=MESH)
    for k in range(1, 4):
        xx = (x + k) % 4

        @pl.when(xx // 2 != xh)
        def _():
            pl.semaphore_signal(barrier, inc=1, device_id=xdev(k), device_id_type=MESH)

    def half(s):
        return og_hbm.at[:, pl.ds(pl.multiple_of(s * 256, 256), 256)]

    my_b = head
    rows_r = pl.ds(pl.multiple_of(rep * 256, 256), 256)
    local = [pltpu.make_async_copy(a, b, lsem.at[n]) for n, (a, b) in enumerate((
        (sb_hbm, sb_ref), (k_hbm, k_ref), (v_hbm, v_ref), (q_hbm, q_ref),
        (half(xl), ogg.at[0, my_b, xl]), (ow_hbm, owg.at[z])))]
    for c in local:
        c.start()

    hd = hadamard()
    hb = hd.astype(BF16)

    def mixing(i):
        for blk in range(2):
            s = [sb_ref[n, i:i + 1, blk * DH:(blk + 1) * DH].astype(F32) * 2.0 - 1.0 for n in range(3)]
            inner = dot_nn((hd * s[1]).astype(BF16), hb).astype(BF16)
            w = dot_nn((hd * s[0]).astype(BF16), inner) * (s[2] * (1.0 / DH))
            hi = w.astype(BF16)
            lo = (w - hi.astype(F32)).astype(BF16)
            wc[i, blk * DH:(blk + 1) * DH, 0:DH] = hi
            wc[i, blk * DH:(blk + 1) * DH, DH:2 * DH] = lo

    local[0].wait()
    for i in range(HL):
        mixing(i)

    def features(x_ref, i):
        xb = x_ref[:, head_cols(i)]
        xf = xb.astype(F32)
        proj = dot_nt(jnp.concatenate([xb, xb], axis=1), wc[i]) * C
        norm = jnp.sum(xf * xf, axis=-1, keepdims=True) * (0.5 * C * C)
        return jnp.exp(proj - norm) * (1.0 / 16.0)

    def put_row(buf, i, row):
        buf[2 * i:2 * i + 1, :] = row[:, 0:DH]
        buf[2 * i + 1:2 * i + 2, :] = row[:, DH:2 * DH]

    def get_row(value, i):
        return jnp.concatenate([value[2 * i:2 * i + 1], value[2 * i + 1:2 * i + 2]], axis=1)

    local[1].wait()
    local[2].wait()
    for i in range(HL):
        p = features(k_ref, i)
        pk[i] = p
        kb = p.astype(BF16)
        kf[i] = kb
        st[i] = dot_tn(kb, v_ref[:, head_cols(i)]).astype(BF16)
        put_row(zs, i, jnp.sum(kb.astype(F32), axis=0, keepdims=True))

    g4, m4 = ctx // 4, ctx % 4

    def member(d):
        return (m4 + d) % 4

    def l1_copy(src, dst, n, d):
        return rcopy(src.at[member(d)], dst.at[d], n + d, {"ctx": g4 * 4 + member(d)})

    def l2_copy(src, dst, n, d, sign):
        return rcopy(src, dst.at[d], n + 3 + d, {"ctx": (ctx + sign * 4 * d + NC) % NC})

    def l3_copy(src, dst, n, d):
        return rcopy(src.at[member(d)], dst.at[m4], n + 6 + d, {"ctx": g4 * 4 + member(d)})

    def group_has(d, sign):
        return g4 + d < 4 if sign > 0 else g4 >= d

    def l1_send(src, dst, n, h):
        for d in (1, 3, 2):
            @pl.when(member(d) // 2 == h)
            def _():
                l1_copy(src, dst, n, d).start()

    def l1_turn(src, buf, total, buf2, n, sign):
        buf[0] = src[m4]
        for d in (1, 3, 2):
            l1_copy(src, buf, n, d).wait_recv()
        total[...] = (buf[0].astype(F32) + buf[1].astype(F32)
                      + buf[2].astype(F32) + buf[3].astype(F32)).astype(BF16)
        for d in (1, 3, 2):
            @pl.when(group_has(d, sign))
            def _():
                l2_copy(total, buf2, n, d, sign).start()

    def l2_turn(buf, total, buf2, obuf, dst, n, sign):
        run[...] = jnp.zeros_like(run)
        for d in (1, 3, 2):
            @pl.when(group_has(d, -sign))
            def _():
                l2_copy(total, buf2, n, d, sign).wait_recv()
                run[...] += buf2[d].astype(F32)
        total_run = run[...]
        for c in (range(4) if sign > 0 else range(3, -1, -1)):
            obuf[c] = total_run.astype(BF16)
            total_run = total_run + buf[(m4 + 4 - c) % 4].astype(F32)
        for d in (1, 3, 2):
            l3_copy(obuf, dst, n, d).start()
        dst[m4] = obuf[m4]

    def l3_done(obuf, dst, n):
        for d in (1, 3, 2):
            l3_copy(obuf, dst, n, d).wait_recv()

    def scan_sent(src, buf, total, buf2, obuf, dst, n, sign):
        for d in (1, 2, 3):
            l1_copy(src, buf, n, d).wait_send()
            l3_copy(obuf, dst, n, d).wait_send()

            @pl.when(group_has(d, sign))
            def _():
                l2_copy(total, buf2, n, d, sign).wait_send()

    def row_copy(src, dst, n, d, sign):
        return rcopy(src, dst.at[d], n + d, {"ctx": (ctx + sign * d + NC) % NC})

    def each(count, fn):
        lax.fori_loop(1, count + 1, lambda d, _: (fn(d), 0)[1], 0)

    pl.semaphore_wait(barrier, 21)

    later, earlier = NC - 1 - ctx, ctx
    each(later, lambda d: row_copy(zs, zr, ZB, d, 1).start())
    l1_send(st, l1, D1, 0)
    l1_send(st, l1, D1, 1)

    ax = {}
    for k in (1, 3, 2):
        xx = (x + k) % 4
        ax[k] = rcopy(half(xx % 2), ogg.at[0, my_b, xl], AX + k, xdev(k))
        ax[k].start()

    def piece(n, k, side=0):
        yy, xx = (y + n) % 4, (x + 4 - k) % 4
        return ogg.at[side, yy * 2 + xx // 2, xx % 2]

    ayp, aym, ay2, ac = {}, {}, {}, {}

    def y_send(k):
        p = piece(0, k)
        src = half(xl) if k == 0 else p
        ayp[k] = rcopy(src, p, AYP + k, yp)
        aym[k] = rcopy(src, p, AYM + k, ym)
        ayp[k].start()
        aym[k].start()

    def a_got(n, k):
        p = piece(n, k)
        if n == 0:
            if k > 0:
                ax[k].wait_recv()
                y_send(k)
            else:
                local[4].wait()
        elif n == 2:
            ay2[k].wait_recv()
        else:
            (ayp if n == 3 else aym)[k].wait_recv()
            if (n == 3) == (k < 2):
                ay2[k] = rcopy(p, p, AY2 + k, yp if n == 3 else ym)
                ay2[k].start()
        c = rcopy(p, piece(n, k, 1), AC + 4 * n + k, sib)
        c.start()
        ac[n, k] = c

    y_send(0)

    bzp, bzm, bc = [], [], []

    def z_send(s, up):
        blk = (z + NZ - s) % NZ if up else (z + s) % NZ
        ref = owg.at[blk, rows_r]
        c = rcopy(ow_hbm.at[rows_r] if s == 0 else ref, ref,
                  (BZP if up else BZM) + s, zp if up else zm)
        c.start()
        (bzp if up else bzm).append(c)

    def b_recv(s, up):
        (bzp if up else bzm)[s].wait_recv()
        blk = (z + NZ - 1 - s) % NZ if up else (z + 1 + s) % NZ
        ref = owg.at[blk, rows_r]
        if s + 1 < (4 if up else 3):
            z_send(s + 1, up)
        c = rcopy(ref, ref, BC + (s if up else 4 + s), sib)
        c.start()
        bc.append(c)

    z_send(0, True)
    z_send(0, False)

    tri = (lax.broadcasted_iota(jnp.int32, (T, T), 0)
           >= lax.broadcasted_iota(jnp.int32, (T, T), 1))

    def q_phase(i):
        p = features(q_ref, i)
        pq[i] = p
        qb = p.astype(BF16)
        qf[i] = qb
        am = jnp.where(tri, dot_nt(qb, kf[i]), 0.0)
        rs[i] = jnp.sum(am, axis=-1, keepdims=True)
        amb = am.astype(BF16)
        ab[i] = amb
        nv[i] = dot_nn(amb, v_ref[:, head_cols(i)])

    atp = []
    ats = rcopy(at.at[pl.ds((1 - rep) * 2, 2)], atg.at[1, xl], ATS, sib)

    def attn_chunk(h):
        for i in (2 * h, 2 * h + 1):
            a = (nv[i] + dot_nn(qf[i], pr[i])) * rd[i]
            attn[i] = a
            at[i] = a.astype(BF16).T
        src = at.at[pl.ds(h * 2, 2)]
        c = rcopy(src, atg.at[(rep + h) % 2, xl], ATP + (rep + h) % 2, {"ctx": pair_ctx, "rep": h})
        c.start()
        atp.append(c)

        @pl.when(rep != h)
        def _():
            ats.start()

        @pl.when(rep == h)
        def _():
            atg[0, xl] = at[h * 2:h * 2 + 2]

    local[3].wait()
    q_phase(0)
    q_phase(1)
    a_got(0, 0)
    a_got(3, 0)
    a_got(0, 1)
    a_got(0, 3)
    q_phase(2)
    b_recv(0, True)
    b_recv(0, False)
    q_phase(3)
    l1_turn(st, l1, tot, l2, D1, 1)
    a_got(0, 2)

    each(earlier, lambda d: row_copy(zs, zr, ZB, d, 1).wait_recv())
    zsum = lax.fori_loop(1, ctx + 1, lambda d, a: a + zr[d], jnp.zeros((8, DH), F32))
    zpre[...] = zsum
    for i in range(HL):
        den = rs[i] + jnp.sum(qf[i].astype(F32) * get_row(zsum, i), axis=-1, keepdims=True)
        rd[i] = 1.0 / den

    b_recv(1, True)
    b_recv(1, False)
    l2_turn(l1, tot, l2, pf, pr, D1, 1)
    a_got(1, 0)
    a_got(3, 1)
    a_got(1, 3)
    b_recv(2, True)
    b_recv(2, False)
    l3_done(pf, pr, D1)
    attn_chunk(0)
    a_got(1, 2)
    a_got(1, 1)
    a_got(3, 3)
    b_recv(3, True)
    attn_chunk(1)
    local[5].wait()

    def go_part(mine):
        tok = xl if mine else 1 - xl

        def tile(m, _):
            rows = pl.ds(pl.multiple_of(m * 128, 128), 128)
            acc = dot_nt(ogg[0, 0, tok, rows, :], owg[0])
            for b in range(1, 8):
                acc += dot_nt(ogg[0, b, tok, rows, :], owg[b])
            if mine:
                gacc[rows, :] = acc
            else:
                gsend[rows, :] = acc.astype(BF16)
            return 0

        lax.fori_loop(0, 2, tile, 0)

    for c in bc:
        c.wait_recv()
    a_got(2, 1)
    a_got(2, 3)
    go_part(False)
    gx = rcopy(gsend, grecv, GX, pair)
    gx.start()

    a_got(3, 2)
    a_got(2, 0)
    a_got(2, 2)
    go_part(True)

    ats.wait_recv()
    for n in range(2):
        rcopy(atg.at[n, xl], atg.at[n, xl], ATP + n, pair).wait_recv()
    for c in ac.values():
        c.wait_recv()

    def w_block(b, ch):
        out = None
        for s in range(2):
            for t in range(2):
                d = dot_nn(atg[s, t, ch], ogg[s, b, t])
                out = d if out is None else out + d
        return out

    cp, cm = {}, {}

    def c_step(s, ch, up):
        sb, rb, cc = (cps, crp, cp) if up else (cms, crm, cm)
        val = w_block((z + 4 - s) % NZ if up else (z + 5 + s) % NZ, ch)
        if s > 0:
            cc[s - 1, ch].wait_recv()
            val += rb[s - 1, ch].astype(F32)
        sb[s, ch] = val.astype(BF16)
        c = rcopy(sb.at[s, ch], rb.at[s, ch], (CP if up else CM) + 2 * s + ch, zp if up else zm)
        c.start()
        cc[s, ch] = c

    def c_round(s):
        for ch in range(2):
            c_step(s, ch, True)
            if s < 3:
                c_step(s, ch, False)

    c_round(0)

    gx.wait_recv()

    def g_chunk(h):
        for i in (2 * h, 2 * h + 1):
            cols = head_cols(i)
            go = gacc[:, cols] + grecv[:, cols].astype(F32)
            r = rd[i]
            gb = (go * r).astype(BF16)
            gnb[i] = gb
            g = -jnp.sum(go * attn[i], axis=-1, keepdims=True) * r
            gd[i] = g
            qb = qf[i]
            st2[i] = dot_tn(qb, gb).astype(BF16)
            put_row(rs2, i, jnp.sum(qb.astype(F32) * g, axis=0, keepdims=True))
        l1_send(st2, l12, D2, h)

    g_chunk(0)
    g_chunk(1)
    each(earlier, lambda d: row_copy(rs2, rr2, RB, d, -1).start())

    def back(i, x_ref, w, out_ref):
        hi = w.astype(BF16)
        lo = (w - hi.astype(F32)).astype(BF16)
        t = dot_nn(hi, wc[i]) + dot_nn(lo, wc[i])
        u = t[:, 0:DH] + t[:, DH:2 * DH]
        xf = x_ref[:, head_cols(i)].astype(F32) * C
        out_ref[:, head_cols(i)] = (C * (u - xf * jnp.sum(w, axis=-1, keepdims=True))).astype(BF16)

    def dq_phase(i):
        gb, g, kb, qb = gnb[i], gd[i], kf[i], qf[i]
        bm = jnp.where(tri, dot_nt(gb, v_ref[:, head_cols(i)]) + g, 0.0).astype(BF16)
        dq = dot_nn(bm, kb) + dot_nt(gb, pr[i]) + g * get_row(zpre[...], i)
        back(i, q_ref, dq * pq[i], qg_ref)
        dk0[i] = dot_tn(bm, qb)
        dv0[i] = dot_tn(ab[i], gb)

    outs = []

    def out(src, dst):
        c = pltpu.make_async_copy(src, dst, lsem.at[6 + len(outs)])
        c.start()
        outs.append(c)

    dq_phase(0)
    c_round(1)
    l1_turn(st2, l12, tot2, l22, D2, -1)
    dq_phase(1)
    c_round(2)
    l2_turn(l12, tot2, l22, pf2, pr2, D2, -1)
    dq_phase(2)
    c_round(3)
    dq_phase(3)
    out(qg_ref, qg_hbm)

    each(later, lambda d: row_copy(rs2, rr2, RB, d, -1).wait_recv())
    rsum = lax.fori_loop(1, later + 1, lambda d, a: a + rr2[d], jnp.zeros((8, DH), F32))

    ccs = []

    def c_last(ch):
        own = w_block(z, ch)
        cp[3, ch].wait_recv()
        cm[2, ch].wait_recv()
        rows = pl.ds(pl.multiple_of(rep * 256 + ch * DH, DH), DH)
        wg_ref[ch] = (own + crp[3, ch].astype(F32) + crm[2, ch].astype(F32)).astype(BF16)
        c = rcopy(wg_ref.at[ch], wg_hbm.at[rows], CC + ch, sib)
        c.start()
        ccs.append(c)
        out(wg_ref.at[ch], wg_hbm.at[rows])

    def dk_chunk(h):
        for i in (2 * h, 2 * h + 1):
            s = pr2[i]
            vb = v_ref[:, head_cols(i)]
            dk = dk0[i] + dot_nt(vb, s) + get_row(rsum, i)
            back(i, k_ref, dk * pk[i], kg_ref)
            vg_ref[:, head_cols(i)] = (dv0[i] + dot_nn(kf[i], s)).astype(BF16)
        cols = slice(h * 256, h * 256 + 256)
        out(kg_ref.at[:, cols], kg_hbm.at[:, cols])
        out(vg_ref.at[:, cols], vg_hbm.at[:, cols])

    l3_done(pf2, pr2, D2)
    dk_chunk(0)
    c_last(0)
    c_last(1)
    dk_chunk(1)

    for group in (ax, ayp, aym, ay2, ac, cp, cm):
        for c in group.values():
            c.wait_send()
    for c in bzp + bzm + bc + atp + [ats, gx]:
        c.wait_send()
    scan_sent(st, l1, tot, l2, pf, pr, D1, 1)
    scan_sent(st2, l12, tot2, l22, pf2, pr2, D2, -1)
    each(later, lambda d: row_copy(zs, zr, ZB, d, 1).wait_send())
    each(earlier, lambda d: row_copy(rs2, rr2, RB, d, -1).wait_send())
    for c in ccs + outs:
        c.wait()


def store(*refs):
    ins, outs, bufs, sem = refs[0:4], refs[4:8], refs[8:12], refs[12]
    load = [pltpu.make_async_copy(a, b, sem.at[i]) for i, (a, b) in enumerate(zip(ins, bufs))]
    save = [pltpu.make_async_copy(a, b, sem.at[4 + i]) for i, (a, b) in enumerate(zip(bufs, outs))]
    for c in load:
        c.start()
    for c, d in zip(load, save):
        c.wait()
        d.start()
    for d in save:
        d.wait()


def on_device(queries, key_vecs, values, out_grad, out_weight, sign_bits):
    flat = lambda a: a.reshape(T, HL * DH)
    hbm = pl.BlockSpec(memory_space=pltpu.HBM)
    state = pltpu.VMEM((HL, M, DH), BF16)
    total = pltpu.VMEM((M, DH), BF16)
    row = pltpu.VMEM((8, DH), F32)
    rows = pltpu.VMEM((NC, 8, DH), F32)
    heads = lambda n, dt: pltpu.VMEM((HL, T, n), dt)
    blocks = lambda n: pltpu.VMEM((n, 2, DH, 256), BF16)
    act = pltpu.VMEM((T, HL * DH), BF16)
    shapes = [jax.ShapeDtypeStruct((T, HL * DH), BF16)] * 3 + [jax.ShapeDtypeStruct((HL * DH, 256), BF16)]
    grads = pl.pallas_call(
        kernel,
        out_shape=shapes,
        in_specs=[hbm] * 6,
        out_specs=[hbm] * 4,
        scratch_shapes=[
            act, act, act, pltpu.VMEM((3, HL, M), jnp.int32),
            act, act, act, pltpu.VMEM((2, DH, 256), BF16),
            pltpu.VMEM((2, 8, 2, T, 256), BF16),
            pltpu.VMEM((NZ, 512, 256), BF16),
            pltpu.VMEM((T, 512), F32),
            act, act,
            state, state, state, total, state, state,
            state, state, state, total, state, state, pltpu.VMEM((M, DH), F32),
            row, rows, row, rows, row,
            heads(256, BF16),
            heads(M, F32), heads(M, F32), heads(M, BF16), heads(M, BF16),
            heads(T, BF16), heads(DH, F32), heads(1, F32), heads(1, F32),
            heads(DH, F32),
            pltpu.VMEM((HL, DH, T), BF16),
            pltpu.VMEM((2, 2, 2, DH, T), BF16),
            heads(DH, BF16), heads(1, F32), heads(M, F32), heads(DH, F32),
            blocks(4), blocks(3), blocks(4), blocks(3),
            pltpu.SemaphoreType.DMA((NSEM,)),
            pltpu.SemaphoreType.DMA((NSEM,)),
            pltpu.SemaphoreType.DMA((13,)),
        ],
        compiler_params=pltpu.CompilerParams(
            collective_id=0, has_side_effects=True, vmem_limit_bytes=62 * 1024 * 1024),
        cost_estimate=pl.CostEstimate(
            flops=5 * 10**9, bytes_accessed=4 * 10**6, transcendentals=5 * 10**5),
        name="performer_back",
    )(flat(queries), flat(key_vecs), flat(values), flat(out_grad), out_weight, sign_bits.transpose(1, 0, 2))
    qg, kg, vg, wg = pl.pallas_call(
        store,
        out_shape=shapes,
        in_specs=[hbm] * 4,
        out_specs=[hbm] * 4,
        scratch_shapes=[act, act, act, pltpu.VMEM((HL * DH, 256), BF16), pltpu.SemaphoreType.DMA((8,))],
        compiler_params=pltpu.CompilerParams(vmem_limit_bytes=62 * 1024 * 1024),
        name="store",
    )(*grads)
    shaped = lambda a: a.reshape(1, T, HL * DH)
    return shaped(qg), shaped(kg), shaped(vg), wg


def solution(mesh):
    tok = P("rep", "ctx", "head")
    return jax.shard_map(
        on_device, mesh=mesh,
        in_specs=(tok, tok, tok, tok, P("head", "ctx"), P("head", None, None)),
        out_specs=(tok, tok, tok, P("head", "ctx")),
        check_vma=False,
    )
```

```python
import functools

import jax
import jax.numpy as jnp
from jax import lax
from jax.experimental import pallas as pl
from jax.experimental.pallas import tpu as pltpu
from jax.sharding import PartitionSpec as P

DH = 128
M = 256
T = 256
HL = 4
NZ = 8
NC = 16
C = DH ** (-0.25)
F32 = jnp.float32
BF16 = jnp.bfloat16
MESH = pl.DeviceIdType.MESH

AX, AYP, AYM, AY2, AC = 0, 4, 8, 12, 16
BZP, BZM, BC = 32, 36, 39
GX, ATS, ATP = 46, 47, 48
CP, CM, CC = 50, 58, 64
D1, D2 = 65, 74
ZB, RB = 83, 98
NSEM = 114


def dot_nn(a, b):
    return lax.dot_general(a, b, (((1,), (0,)), ((), ())), preferred_element_type=F32)


def dot_nt(a, b):
    return lax.dot_general(a, b, (((1,), (1,)), ((), ())), preferred_element_type=F32)


def dot_tn(a, b):
    return lax.dot_general(a, b, (((0,), (0,)), ((), ())), preferred_element_type=F32)


def hadamard():
    i = lax.broadcasted_iota(jnp.int32, (DH, DH), 0)
    j = lax.broadcasted_iota(jnp.int32, (DH, DH), 1)
    x = i & j
    x = x ^ (x >> 4)
    x = x ^ (x >> 2)
    x = x ^ (x >> 1)
    return (1 - 2 * (x & 1)).astype(F32)


def head_cols(i):
    return pl.ds(pl.multiple_of(i * DH, DH), DH)


def kernel(q_hbm, k_hbm, v_hbm, og_hbm, ow_hbm, sb_hbm,
           qg_hbm, kg_hbm, vg_hbm, wg_hbm,
           q_ref, k_ref, v_ref, sb_ref, qg_ref, kg_ref, vg_ref, wg_ref,
           ogg, owg, gacc, gsend, grecv,
           st, l1, l2, tot, pf, pr, st2, l12, l22, tot2, pf2, pr2, run, zs, zr, rs2, rr2, zpre,
           wc, pq, pk, qf, kf, ab, nv, rs, rd, attn, at, atg,
           gnb, gd, dk0, dv0, wpre, cps, cms, crp, crm,
           ssem, rsem, lsem):
    ctx = lax.axis_index("ctx")
    head = lax.axis_index("head")
    rep = lax.axis_index("rep")
    z, xl = ctx // 2, ctx % 2
    y, xh = head // 2, head % 2
    x = xh * 2 + xl
    sib = {"rep": 1 - rep}
    pair_ctx = z * 2 + 1 - xl
    pair = {"ctx": pair_ctx}
    pair_sib = {"ctx": pair_ctx, "rep": 1 - rep}
    yp = {"head": (head + 2) % 8}
    ym = {"head": (head + 6) % 8}
    zp = {"ctx": (ctx + 2) % NC}
    zm = {"ctx": (ctx + NC - 2) % NC}

    def xdev(k):
        xx = (x + k) % 4
        return {"ctx": z * 2 + xx % 2, "head": y * 2 + xx // 2}

    def rcopy(src, dst, n, dev):
        return pltpu.make_async_remote_copy(
            src_ref=src, dst_ref=dst, send_sem=ssem.at[n], recv_sem=rsem.at[n],
            device_id=dev, device_id_type=MESH)

    barrier = pltpu.get_barrier_semaphore()

    def greet(d, _):
        pl.semaphore_signal(barrier, inc=1, device_id={"ctx": (ctx + d) % NC}, device_id_type=MESH)
        return 0

    lax.fori_loop(1, NC, greet, 0)
    for dev in (sib, pair_sib, yp, ym):
        pl.semaphore_signal(barrier, inc=1, device_id=dev, device_id_type=MESH)
    for k in range(1, 4):
        xx = (x + k) % 4

        @pl.when(xx // 2 != xh)
        def _():
            pl.semaphore_signal(barrier, inc=1, device_id=xdev(k), device_id_type=MESH)

    def half(s):
        return og_hbm.at[:, pl.ds(pl.multiple_of(s * 256, 256), 256)]

    my_b = head
    rows_r = pl.ds(pl.multiple_of(rep * 256, 256), 256)
    local = [pltpu.make_async_copy(a, b, lsem.at[n]) for n, (a, b) in enumerate((
        (sb_hbm, sb_ref), (k_hbm, k_ref), (v_hbm, v_ref), (q_hbm, q_ref),
        (half(xl), ogg.at[0, my_b, xl]), (ow_hbm, owg.at[z])))]
    for c in local:
        c.start()

    hd = hadamard()
    hb = hd.astype(BF16)

    def mixing(i):
        for blk in range(2):
            s = [sb_ref[n, i:i + 1, blk * DH:(blk + 1) * DH].astype(F32) * 2.0 - 1.0 for n in range(3)]
            inner = dot_nn((hd * s[1]).astype(BF16), hb).astype(BF16)
            w = dot_nn((hd * s[0]).astype(BF16), inner) * (s[2] * (1.0 / DH))
            hi = w.astype(BF16)
            lo = (w - hi.astype(F32)).astype(BF16)
            wc[i, blk * DH:(blk + 1) * DH, 0:DH] = hi
            wc[i, blk * DH:(blk + 1) * DH, DH:2 * DH] = lo

    local[0].wait()
    for i in range(HL):
        mixing(i)

    def features(x_ref, i):
        xb = x_ref[:, head_cols(i)]
        xf = xb.astype(F32)
        proj = dot_nt(jnp.concatenate([xb, xb], axis=1), wc[i]) * C
        norm = jnp.sum(xf * xf, axis=-1, keepdims=True) * (0.5 * C * C)
        return jnp.exp(proj - norm) * (1.0 / 16.0)

    def put_row(buf, i, row):
        buf[2 * i:2 * i + 1, :] = row[:, 0:DH]
        buf[2 * i + 1:2 * i + 2, :] = row[:, DH:2 * DH]

    def get_row(value, i):
        return jnp.concatenate([value[2 * i:2 * i + 1], value[2 * i + 1:2 * i + 2]], axis=1)

    local[1].wait()
    local[2].wait()
    for i in range(HL):
        p = features(k_ref, i)
        pk[i] = p
        kb = p.astype(BF16)
        kf[i] = kb
        st[i] = dot_tn(kb, v_ref[:, head_cols(i)]).astype(BF16)
        put_row(zs, i, jnp.sum(kb.astype(F32), axis=0, keepdims=True))

    g4, m4 = ctx // 4, ctx % 4

    def member(d):
        return (m4 + d) % 4

    def l1_copy(src, dst, n, d):
        return rcopy(src.at[member(d)], dst.at[d], n + d, {"ctx": g4 * 4 + member(d)})

    def l2_copy(src, dst, n, d, sign):
        return rcopy(src, dst.at[d], n + 3 + d, {"ctx": (ctx + sign * 4 * d + NC) % NC})

    def l3_copy(src, dst, n, d):
        return rcopy(src.at[member(d)], dst.at[m4], n + 6 + d, {"ctx": g4 * 4 + member(d)})

    def group_has(d, sign):
        return g4 + d < 4 if sign > 0 else g4 >= d

    def l1_send(src, dst, n, h):
        for d in (1, 3, 2):
            @pl.when(member(d) // 2 == h)
            def _():
                l1_copy(src, dst, n, d).start()

    def l1_turn(src, buf, total, buf2, n, sign):
        buf[0] = src[m4]
        for d in (1, 3, 2):
            l1_copy(src, buf, n, d).wait_recv()
        total[...] = (buf[0].astype(F32) + buf[1].astype(F32)
                      + buf[2].astype(F32) + buf[3].astype(F32)).astype(BF16)
        for d in (1, 3, 2):
            @pl.when(group_has(d, sign))
            def _():
                l2_copy(total, buf2, n, d, sign).start()

    def l2_turn(buf, total, buf2, obuf, dst, n, sign):
        run[...] = jnp.zeros_like(run)
        for d in (1, 3, 2):
            @pl.when(group_has(d, -sign))
            def _():
                l2_copy(total, buf2, n, d, sign).wait_recv()
                run[...] += buf2[d].astype(F32)
        total_run = run[...]
        for c in (range(4) if sign > 0 else range(3, -1, -1)):
            obuf[c] = total_run.astype(BF16)
            total_run = total_run + buf[(m4 + 4 - c) % 4].astype(F32)
        for d in (1, 3, 2):
            l3_copy(obuf, dst, n, d).start()
        dst[m4] = obuf[m4]

    def l3_done(obuf, dst, n):
        for d in (1, 3, 2):
            l3_copy(obuf, dst, n, d).wait_recv()

    def scan_sent(src, buf, total, buf2, obuf, dst, n, sign):
        for d in (1, 2, 3):
            l1_copy(src, buf, n, d).wait_send()
            l3_copy(obuf, dst, n, d).wait_send()

            @pl.when(group_has(d, sign))
            def _():
                l2_copy(total, buf2, n, d, sign).wait_send()

    def row_copy(src, dst, n, d, sign):
        return rcopy(src, dst.at[d], n + d, {"ctx": (ctx + sign * d + NC) % NC})

    def each(count, fn):
        lax.fori_loop(1, count + 1, lambda d, _: (fn(d), 0)[1], 0)

    pl.semaphore_wait(barrier, 21)

    later, earlier = NC - 1 - ctx, ctx
    each(later, lambda d: row_copy(zs, zr, ZB, d, 1).start())

    ax = {}
    for k in (1, 3, 2):
        xx = (x + k) % 4
        ax[k] = rcopy(half(xx % 2), ogg.at[0, my_b, xl], AX + k, xdev(k))
        ax[k].start()

    def piece(n, k, side=0):
        yy, xx = (y + n) % 4, (x + 4 - k) % 4
        return ogg.at[side, yy * 2 + xx // 2, xx % 2]

    ayp, aym, ay2, ac = {}, {}, {}, {}

    def y_send(k):
        p = piece(0, k)
        src = half(xl) if k == 0 else p
        ayp[k] = rcopy(src, p, AYP + k, yp)
        aym[k] = rcopy(src, p, AYM + k, ym)
        ayp[k].start()
        aym[k].start()

    def a_got(n, k):
        p = piece(n, k)
        if n == 0:
            if k > 0:
                ax[k].wait_recv()
                y_send(k)
            else:
                local[4].wait()
        elif n == 2:
            ay2[k].wait_recv()
        else:
            (ayp if n == 3 else aym)[k].wait_recv()
            if (n == 3) == (k < 2):
                ay2[k] = rcopy(p, p, AY2 + k, yp if n == 3 else ym)
                ay2[k].start()
        c = rcopy(p, piece(n, k, 1), AC + 4 * n + k, sib)
        c.start()
        ac[n, k] = c

    y_send(0)

    bzp, bzm, bc = [], [], []

    def z_send(s, up):
        blk = (z + NZ - s) % NZ if up else (z + s) % NZ
        ref = owg.at[blk, rows_r]
        c = rcopy(ow_hbm.at[rows_r] if s == 0 else ref, ref,
                  (BZP if up else BZM) + s, zp if up else zm)
        c.start()
        (bzp if up else bzm).append(c)

    def b_recv(s, up):
        (bzp if up else bzm)[s].wait_recv()
        blk = (z + NZ - 1 - s) % NZ if up else (z + 1 + s) % NZ
        ref = owg.at[blk, rows_r]
        if s + 1 < (4 if up else 3):
            z_send(s + 1, up)
        c = rcopy(ref, ref, BC + (s if up else 4 + s), sib)
        c.start()
        bc.append(c)

    z_send(0, True)
    z_send(0, False)
    l1_send(st, l1, D1, 0)
    l1_send(st, l1, D1, 1)

    tri = (lax.broadcasted_iota(jnp.int32, (T, T), 0)
           >= lax.broadcasted_iota(jnp.int32, (T, T), 1))

    def q_phase(i):
        p = features(q_ref, i)
        pq[i] = p
        qb = p.astype(BF16)
        qf[i] = qb
        am = jnp.where(tri, dot_nt(qb, kf[i]), 0.0)
        rs[i] = jnp.sum(am, axis=-1, keepdims=True)
        amb = am.astype(BF16)
        ab[i] = amb
        nv[i] = dot_nn(amb, v_ref[:, head_cols(i)])

    atp = []
    ats = rcopy(at.at[pl.ds((1 - rep) * 2, 2)], atg.at[1, xl], ATS, sib)

    def attn_chunk(h):
        for i in (2 * h, 2 * h + 1):
            a = (nv[i] + dot_nn(qf[i], pr[i])) * rd[i]
            attn[i] = a
            at[i] = a.astype(BF16).T
        src = at.at[pl.ds(h * 2, 2)]
        c = rcopy(src, atg.at[(rep + h) % 2, xl], ATP + (rep + h) % 2, {"ctx": pair_ctx, "rep": h})
        c.start()
        atp.append(c)

        @pl.when(rep != h)
        def _():
            ats.start()

        @pl.when(rep == h)
        def _():
            atg[0, xl] = at[h * 2:h * 2 + 2]

    local[3].wait()
    q_phase(0)
    q_phase(1)
    a_got(0, 0)
    a_got(3, 0)
    a_got(0, 1)
    a_got(0, 3)
    b_recv(0, True)
    b_recv(0, False)
    q_phase(2)
    l1_turn(st, l1, tot, l2, D1, 1)
    b_recv(1, True)
    b_recv(1, False)
    a_got(0, 2)
    q_phase(3)

    each(earlier, lambda d: row_copy(zs, zr, ZB, d, 1).wait_recv())
    zsum = lax.fori_loop(1, ctx + 1, lambda d, a: a + zr[d], jnp.zeros((8, DH), F32))
    zpre[...] = zsum
    for i in range(HL):
        den = rs[i] + jnp.sum(qf[i].astype(F32) * get_row(zsum, i), axis=-1, keepdims=True)
        rd[i] = 1.0 / den

    a_got(1, 0)
    a_got(3, 1)
    l2_turn(l1, tot, l2, pf, pr, D1, 1)
    a_got(1, 3)
    b_recv(2, True)
    b_recv(2, False)
    l3_done(pf, pr, D1)
    attn_chunk(0)
    a_got(1, 2)
    a_got(1, 1)
    a_got(3, 3)
    b_recv(3, True)
    attn_chunk(1)
    local[5].wait()

    def go_part(mine):
        tok = xl if mine else 1 - xl

        def tile(m, _):
            rows = pl.ds(pl.multiple_of(m * 128, 128), 128)
            acc = dot_nt(ogg[0, 0, tok, rows, :], owg[0])
            for b in range(1, 8):
                acc += dot_nt(ogg[0, b, tok, rows, :], owg[b])
            if mine:
                gacc[rows, :] = acc
            else:
                gsend[rows, :] = acc.astype(BF16)
            return 0

        lax.fori_loop(0, 2, tile, 0)

    for c in bc:
        c.wait_recv()
    a_got(2, 1)
    a_got(2, 3)
    go_part(False)
    gx = rcopy(gsend, grecv, GX, pair)
    gx.start()

    a_got(3, 2)
    a_got(2, 0)
    a_got(2, 2)
    ats.wait_recv()
    for n in range(2):
        rcopy(atg.at[n, xl], atg.at[n, xl], ATP + n, pair).wait_recv()
    for c in ac.values():
        c.wait_recv()

    def w_block(b, ch):
        out = None
        for s in range(2):
            for t in range(2):
                d = dot_nn(atg[s, t, ch], ogg[s, b, t])
                out = d if out is None else out + d
        return out

    cp, cm = {}, {}

    def c_ready(s):
        for ch in range(2):
            if s < 4:
                wpre[0, ch] = w_block((z + 4 - s) % NZ, ch)
                if s < 3:
                    wpre[1, ch] = w_block((z + 5 + s) % NZ, ch)
            else:
                wpre[0, ch] = w_block(z, ch)

    def c_step(s, ch, up):
        sb, rb, cc = (cps, crp, cp) if up else (cms, crm, cm)
        if s == 0:
            val = w_block((z + 4) % NZ if up else (z + 5) % NZ, ch)
        else:
            val = wpre[0 if up else 1, ch]
            cc[s - 1, ch].wait_recv()
            val += rb[s - 1, ch].astype(F32)
        sb[s, ch] = val.astype(BF16)
        c = rcopy(sb.at[s, ch], rb.at[s, ch], (CP if up else CM) + 2 * s + ch, zp if up else zm)
        c.start()
        cc[s, ch] = c

    def c_round(s):
        for ch in range(2):
            c_step(s, ch, True)
            if s < 3:
                c_step(s, ch, False)

    c_round(0)
    go_part(True)
    c_ready(1)

    gx.wait_recv()

    def g_chunk(h):
        for i in (2 * h, 2 * h + 1):
            cols = head_cols(i)
            go = gacc[:, cols] + grecv[:, cols].astype(F32)
            r = rd[i]
            gb = (go * r).astype(BF16)
            gnb[i] = gb
            g = -jnp.sum(go * attn[i], axis=-1, keepdims=True) * r
            gd[i] = g
            qb = qf[i]
            st2[i] = dot_tn(qb, gb).astype(BF16)
            put_row(rs2, i, jnp.sum(qb.astype(F32) * g, axis=0, keepdims=True))
        l1_send(st2, l12, D2, h)

    g_chunk(0)
    g_chunk(1)
    each(earlier, lambda d: row_copy(rs2, rr2, RB, d, -1).start())

    def back(i, x_ref, w, out_ref):
        hi = w.astype(BF16)
        lo = (w - hi.astype(F32)).astype(BF16)
        t = dot_nn(hi, wc[i]) + dot_nn(lo, wc[i])
        u = t[:, 0:DH] + t[:, DH:2 * DH]
        xf = x_ref[:, head_cols(i)].astype(F32) * C
        out_ref[:, head_cols(i)] = (C * (u - xf * jnp.sum(w, axis=-1, keepdims=True))).astype(BF16)

    def dq_phase(i):
        gb, g, kb, qb = gnb[i], gd[i], kf[i], qf[i]
        bm = jnp.where(tri, dot_nt(gb, v_ref[:, head_cols(i)]) + g, 0.0).astype(BF16)
        dq = dot_nn(bm, kb) + dot_nt(gb, pr[i]) + g * get_row(zpre[...], i)
        back(i, q_ref, dq * pq[i], qg_ref)
        dk0[i] = dot_tn(bm, qb)
        dv0[i] = dot_tn(ab[i], gb)

    outs = []

    def out(src, dst):
        c = pltpu.make_async_copy(src, dst, lsem.at[6 + len(outs)])
        c.start()
        outs.append(c)

    c_round(1)
    c_ready(2)
    dq_phase(0)
    l1_turn(st2, l12, tot2, l22, D2, -1)
    c_round(2)
    c_ready(3)
    dq_phase(1)
    l2_turn(l12, tot2, l22, pf2, pr2, D2, -1)
    c_round(3)
    c_ready(4)
    dq_phase(2)
    dq_phase(3)
    out(qg_ref, qg_hbm)

    each(later, lambda d: row_copy(rs2, rr2, RB, d, -1).wait_recv())
    rsum = lax.fori_loop(1, later + 1, lambda d, a: a + rr2[d], jnp.zeros((8, DH), F32))

    ccs = []

    def c_last(ch):
        own = wpre[0, ch]
        cp[3, ch].wait_recv()
        cm[2, ch].wait_recv()
        rows = pl.ds(pl.multiple_of(rep * 256 + ch * DH, DH), DH)
        wg_ref[ch] = (own + crp[3, ch].astype(F32) + crm[2, ch].astype(F32)).astype(BF16)
        c = rcopy(wg_ref.at[ch], wg_hbm.at[rows], CC + ch, sib)
        c.start()
        ccs.append(c)
        out(wg_ref.at[ch], wg_hbm.at[rows])

    def dk_chunk(h):
        for i in (2 * h, 2 * h + 1):
            s = pr2[i]
            vb = v_ref[:, head_cols(i)]
            dk = dk0[i] + dot_nt(vb, s) + get_row(rsum, i)
            back(i, k_ref, dk * pk[i], kg_ref)
            vg_ref[:, head_cols(i)] = (dv0[i] + dot_nn(kf[i], s)).astype(BF16)
        cols = slice(h * 256, h * 256 + 256)
        out(kg_ref.at[:, cols], kg_hbm.at[:, cols])
        out(vg_ref.at[:, cols], vg_hbm.at[:, cols])

    l3_done(pf2, pr2, D2)
    dk_chunk(0)
    c_last(0)
    c_last(1)
    dk_chunk(1)

    for group in (ax, ayp, aym, ay2, ac, cp, cm):
        for c in group.values():
            c.wait_send()
    for c in bzp + bzm + bc + atp + [ats, gx]:
        c.wait_send()
    scan_sent(st, l1, tot, l2, pf, pr, D1, 1)
    scan_sent(st2, l12, tot2, l22, pf2, pr2, D2, -1)
    each(later, lambda d: row_copy(zs, zr, ZB, d, 1).wait_send())
    each(earlier, lambda d: row_copy(rs2, rr2, RB, d, -1).wait_send())
    for c in ccs + outs:
        c.wait()


def store(*refs):
    ins, outs, bufs, sem = refs[0:4], refs[4:8], refs[8:12], refs[12]
    load = [pltpu.make_async_copy(a, b, sem.at[i]) for i, (a, b) in enumerate(zip(ins, bufs))]
    save = [pltpu.make_async_copy(a, b, sem.at[4 + i]) for i, (a, b) in enumerate(zip(bufs, outs))]
    for c in load:
        c.start()
    for c, d in zip(load, save):
        c.wait()
        d.start()
    for d in save:
        d.wait()


def on_device(queries, key_vecs, values, out_grad, out_weight, sign_bits):
    flat = lambda a: a.reshape(T, HL * DH)
    hbm = pl.BlockSpec(memory_space=pltpu.HBM)
    state = pltpu.VMEM((HL, M, DH), BF16)
    total = pltpu.VMEM((M, DH), BF16)
    row = pltpu.VMEM((8, DH), F32)
    rows = pltpu.VMEM((NC, 8, DH), F32)
    heads = lambda n, dt: pltpu.VMEM((HL, T, n), dt)
    blocks = lambda n: pltpu.VMEM((n, 2, DH, 256), BF16)
    act = pltpu.VMEM((T, HL * DH), BF16)
    shapes = [jax.ShapeDtypeStruct((T, HL * DH), BF16)] * 3 + [jax.ShapeDtypeStruct((HL * DH, 256), BF16)]
    grads = pl.pallas_call(
        kernel,
        out_shape=shapes,
        in_specs=[hbm] * 6,
        out_specs=[hbm] * 4,
        scratch_shapes=[
            act, act, act, pltpu.VMEM((3, HL, M), jnp.int32),
            act, act, act, pltpu.VMEM((2, DH, 256), BF16),
            pltpu.VMEM((2, 8, 2, T, 256), BF16),
            pltpu.VMEM((NZ, 512, 256), BF16),
            pltpu.VMEM((T, 512), F32),
            act, act,
            state, state, state, total, state, state,
            state, state, state, total, state, state, pltpu.VMEM((M, DH), F32),
            row, rows, row, rows, row,
            heads(256, BF16),
            heads(M, F32), heads(M, F32), heads(M, BF16), heads(M, BF16),
            heads(T, BF16), heads(DH, F32), heads(1, F32), heads(1, F32),
            heads(DH, F32),
            pltpu.VMEM((HL, DH, T), BF16),
            pltpu.VMEM((2, 2, 2, DH, T), BF16),
            heads(DH, BF16), heads(1, F32), heads(M, F32), heads(DH, F32),
            pltpu.VMEM((2, 2, DH, 256), F32), blocks(4), blocks(3), blocks(4), blocks(3),
            pltpu.SemaphoreType.DMA((NSEM,)),
            pltpu.SemaphoreType.DMA((NSEM,)),
            pltpu.SemaphoreType.DMA((13,)),
        ],
        compiler_params=pltpu.CompilerParams(
            collective_id=0, has_side_effects=True, vmem_limit_bytes=62 * 1024 * 1024),
        cost_estimate=pl.CostEstimate(
            flops=5 * 10**9, bytes_accessed=4 * 10**6, transcendentals=5 * 10**5),
        name="performer_back",
    )(flat(queries), flat(key_vecs), flat(values), flat(out_grad), out_weight, sign_bits.transpose(1, 0, 2))
    qg, kg, vg, wg = pl.pallas_call(
        store,
        out_shape=shapes,
        in_specs=[hbm] * 4,
        out_specs=[hbm] * 4,
        scratch_shapes=[act, act, act, pltpu.VMEM((HL * DH, 256), BF16), pltpu.SemaphoreType.DMA((8,))],
        compiler_params=pltpu.CompilerParams(vmem_limit_bytes=62 * 1024 * 1024),
        name="store",
    )(*grads)
    shaped = lambda a: a.reshape(1, T, HL * DH)
    return shaped(qg), shaped(kg), shaped(vg), wg


def solution(mesh):
    tok = P("rep", "ctx", "head")
    return jax.shard_map(
        on_device, mesh=mesh,
        in_specs=(tok, tok, tok, tok, P("head", "ctx"), P("head", None, None)),
        out_specs=(tok, tok, tok, P("head", "ctx")),
        check_vma=False,
    )
```

```python
import functools

import jax
import jax.numpy as jnp
from jax import lax
from jax.experimental import pallas as pl
from jax.experimental.pallas import tpu as pltpu
from jax.sharding import PartitionSpec as P

DH = 128
M = 256
T = 256
HL = 4
NZ = 8
NC = 16
C = DH ** (-0.25)
F32 = jnp.float32
BF16 = jnp.bfloat16
MESH = pl.DeviceIdType.MESH

AX, AYP, AYM, AY2, AC = 0, 4, 8, 12, 16
BZP, BZM, BC = 114, 122, 128
GX, ATS, ATP = 46, 47, 48
CP, CM, CC = 50, 58, 64
D1, D2 = 65, 74
ZB, RB = 83, 98
NSEM = 142


def dot_nn(a, b):
    return lax.dot_general(a, b, (((1,), (0,)), ((), ())), preferred_element_type=F32)


def dot_nt(a, b):
    return lax.dot_general(a, b, (((1,), (1,)), ((), ())), preferred_element_type=F32)


def dot_tn(a, b):
    return lax.dot_general(a, b, (((0,), (0,)), ((), ())), preferred_element_type=F32)


def hadamard():
    i = lax.broadcasted_iota(jnp.int32, (DH, DH), 0)
    j = lax.broadcasted_iota(jnp.int32, (DH, DH), 1)
    x = i & j
    x = x ^ (x >> 4)
    x = x ^ (x >> 2)
    x = x ^ (x >> 1)
    return (1 - 2 * (x & 1)).astype(F32)


def head_cols(i):
    return pl.ds(pl.multiple_of(i * DH, DH), DH)


def kernel(q_hbm, k_hbm, v_hbm, og_hbm, ow_hbm, sb_hbm,
           qg_hbm, kg_hbm, vg_hbm, wg_hbm,
           q_ref, k_ref, v_ref, sb_ref, qg_ref, kg_ref, vg_ref, wg_ref,
           ogg, owg, gacc, gsend, grecv,
           st, l1, l2, tot, pf, pr, st2, l12, l22, tot2, pf2, pr2, run, zs, zr, rs2, rr2, zpre,
           wc, pq, pk, qf, kf, ab, nv, rs, rd, attn, at, atg,
           gnb, gd, dk0, dv0, wpre, cps, cms, crp, crm,
           ssem, rsem, lsem):
    ctx = lax.axis_index("ctx")
    head = lax.axis_index("head")
    rep = lax.axis_index("rep")
    z, xl = ctx // 2, ctx % 2
    y, xh = head // 2, head % 2
    x = xh * 2 + xl
    sib = {"rep": 1 - rep}
    pair_ctx = z * 2 + 1 - xl
    pair = {"ctx": pair_ctx}
    pair_sib = {"ctx": pair_ctx, "rep": 1 - rep}
    yp = {"head": (head + 2) % 8}
    ym = {"head": (head + 6) % 8}
    zp = {"ctx": (ctx + 2) % NC}
    zm = {"ctx": (ctx + NC - 2) % NC}

    def xdev(k):
        xx = (x + k) % 4
        return {"ctx": z * 2 + xx % 2, "head": y * 2 + xx // 2}

    def rcopy(src, dst, n, dev):
        return pltpu.make_async_remote_copy(
            src_ref=src, dst_ref=dst, send_sem=ssem.at[n], recv_sem=rsem.at[n],
            device_id=dev, device_id_type=MESH)

    barrier = pltpu.get_barrier_semaphore()

    def greet(d, _):
        pl.semaphore_signal(barrier, inc=1, device_id={"ctx": (ctx + d) % NC}, device_id_type=MESH)
        return 0

    lax.fori_loop(1, NC, greet, 0)
    for dev in (sib, pair_sib, yp, ym):
        pl.semaphore_signal(barrier, inc=1, device_id=dev, device_id_type=MESH)
    for k in range(1, 4):
        xx = (x + k) % 4

        @pl.when(xx // 2 != xh)
        def _():
            pl.semaphore_signal(barrier, inc=1, device_id=xdev(k), device_id_type=MESH)

    def half(s):
        return og_hbm.at[:, pl.ds(pl.multiple_of(s * 256, 256), 256)]

    my_b = head
    local = [pltpu.make_async_copy(a, b, lsem.at[n]) for n, (a, b) in enumerate((
        (sb_hbm, sb_ref), (k_hbm, k_ref), (v_hbm, v_ref), (q_hbm, q_ref),
        (half(xl), ogg.at[0, my_b, xl]), (ow_hbm, owg.at[z])))]
    for c in local:
        c.start()

    hd = hadamard()
    hb = hd.astype(BF16)

    def mixing(i):
        for blk in range(2):
            s = [sb_ref[n, i:i + 1, blk * DH:(blk + 1) * DH].astype(F32) * 2.0 - 1.0 for n in range(3)]
            inner = dot_nn((hd * s[1]).astype(BF16), hb).astype(BF16)
            w = dot_nn((hd * s[0]).astype(BF16), inner) * (s[2] * (1.0 / DH))
            hi = w.astype(BF16)
            lo = (w - hi.astype(F32)).astype(BF16)
            wc[i, blk * DH:(blk + 1) * DH, 0:DH] = hi
            wc[i, blk * DH:(blk + 1) * DH, DH:2 * DH] = lo

    local[0].wait()
    for i in range(HL):
        mixing(i)

    def features(x_ref, i):
        xb = x_ref[:, head_cols(i)]
        xf = xb.astype(F32)
        proj = dot_nt(jnp.concatenate([xb, xb], axis=1), wc[i]) * C
        norm = jnp.sum(xf * xf, axis=-1, keepdims=True) * (0.5 * C * C)
        return jnp.exp(proj - norm) * (1.0 / 16.0)

    def put_row(buf, i, row):
        buf[2 * i:2 * i + 1, :] = row[:, 0:DH]
        buf[2 * i + 1:2 * i + 2, :] = row[:, DH:2 * DH]

    def get_row(value, i):
        return jnp.concatenate([value[2 * i:2 * i + 1], value[2 * i + 1:2 * i + 2]], axis=1)

    local[1].wait()
    local[2].wait()
    for i in range(HL):
        p = features(k_ref, i)
        pk[i] = p
        kb = p.astype(BF16)
        kf[i] = kb
        st[i] = dot_tn(kb, v_ref[:, head_cols(i)]).astype(BF16)
        put_row(zs, i, jnp.sum(kb.astype(F32), axis=0, keepdims=True))

    g4, m4 = ctx // 4, ctx % 4

    def member(d):
        return (m4 + d) % 4

    def l1_copy(src, dst, n, d):
        return rcopy(src.at[member(d)], dst.at[d], n + d, {"ctx": g4 * 4 + member(d)})

    def l2_copy(src, dst, n, d, sign):
        return rcopy(src, dst.at[d], n + 3 + d, {"ctx": (ctx + sign * 4 * d + NC) % NC})

    def l3_copy(src, dst, n, d):
        return rcopy(src.at[member(d)], dst.at[m4], n + 6 + d, {"ctx": g4 * 4 + member(d)})

    def group_has(d, sign):
        return g4 + d < 4 if sign > 0 else g4 >= d

    def l1_send(src, dst, n, h):
        for d in (1, 3, 2):
            @pl.when(member(d) // 2 == h)
            def _():
                l1_copy(src, dst, n, d).start()

    def l1_turn(src, buf, total, buf2, n, sign):
        buf[0] = src[m4]
        for d in (1, 3, 2):
            l1_copy(src, buf, n, d).wait_recv()
        total[...] = (buf[0].astype(F32) + buf[1].astype(F32)
                      + buf[2].astype(F32) + buf[3].astype(F32)).astype(BF16)
        for d in (1, 3, 2):
            @pl.when(group_has(d, sign))
            def _():
                l2_copy(total, buf2, n, d, sign).start()

    def l2_turn(buf, total, buf2, obuf, dst, n, sign):
        run[...] = jnp.zeros_like(run)
        for d in (1, 3, 2):
            @pl.when(group_has(d, -sign))
            def _():
                l2_copy(total, buf2, n, d, sign).wait_recv()
                run[...] += buf2[d].astype(F32)
        total_run = run[...]
        for c in (range(4) if sign > 0 else range(3, -1, -1)):
            obuf[c] = total_run.astype(BF16)
            total_run = total_run + buf[(m4 + 4 - c) % 4].astype(F32)
        for d in (1, 3, 2):
            l3_copy(obuf, dst, n, d).start()
        dst[m4] = obuf[m4]

    def l3_done(obuf, dst, n):
        for d in (1, 3, 2):
            l3_copy(obuf, dst, n, d).wait_recv()

    def scan_sent(src, buf, total, buf2, obuf, dst, n, sign):
        for d in (1, 2, 3):
            l1_copy(src, buf, n, d).wait_send()
            l3_copy(obuf, dst, n, d).wait_send()

            @pl.when(group_has(d, sign))
            def _():
                l2_copy(total, buf2, n, d, sign).wait_send()

    def row_copy(src, dst, n, d, sign):
        return rcopy(src, dst.at[d], n + d, {"ctx": (ctx + sign * d + NC) % NC})

    def each(count, fn):
        lax.fori_loop(1, count + 1, lambda d, _: (fn(d), 0)[1], 0)

    pl.semaphore_wait(barrier, 21)

    later, earlier = NC - 1 - ctx, ctx
    each(later, lambda d: row_copy(zs, zr, ZB, d, 1).start())

    ax = {}
    for k in (1, 3, 2):
        xx = (x + k) % 4
        ax[k] = rcopy(half(xx % 2), ogg.at[0, my_b, xl], AX + k, xdev(k))
        ax[k].start()

    def piece(n, k, side=0):
        yy, xx = (y + n) % 4, (x + 4 - k) % 4
        return ogg.at[side, yy * 2 + xx // 2, xx % 2]

    ayp, aym, ay2, ac = {}, {}, {}, {}

    def y_send(k):
        p = piece(0, k)
        src = half(xl) if k == 0 else p
        ayp[k] = rcopy(src, p, AYP + k, yp)
        aym[k] = rcopy(src, p, AYM + k, ym)
        ayp[k].start()
        aym[k].start()

    def a_got(n, k):
        p = piece(n, k)
        if n == 0:
            if k > 0:
                ax[k].wait_recv()
                y_send(k)
            else:
                local[4].wait()
        elif n == 2:
            ay2[k].wait_recv()
        else:
            (ayp if n == 3 else aym)[k].wait_recv()
            if (n == 3) == (k < 2):
                ay2[k] = rcopy(p, p, AY2 + k, yp if n == 3 else ym)
                ay2[k].start()
        c = rcopy(p, piece(n, k, 1), AC + 4 * n + k, sib)
        c.start()
        ac[n, k] = c

    y_send(0)

    bzp, bzm, bc = {}, {}, []

    def z_rows(h):
        return pl.ds(pl.multiple_of(rep * 256 + h * 128, 128), 128)

    def z_send(s, up, pieces=(0, 1)):
        blk = (z + NZ - s) % NZ if up else (z + s) % NZ
        for h in pieces:
            ref = owg.at[blk, z_rows(h)]
            c = rcopy(ow_hbm.at[z_rows(h)] if s == 0 else ref, ref,
                      (BZP if up else BZM) + 2 * s + h, zp if up else zm)
            c.start()
            (bzp if up else bzm)[s, h] = c

    def b_recv(s, up):
        blk = (z + NZ - 1 - s) % NZ if up else (z + 1 + s) % NZ
        for h in range(2):
            (bzp if up else bzm)[s, h].wait_recv()
            if s + 1 < (4 if up else 3):
                z_send(s + 1, up, (h,))
            ref = owg.at[blk, z_rows(h)]
            c = rcopy(ref, ref, BC + 2 * (s if up else 4 + s) + h, sib)
            c.start()
            bc.append(c)

    z_send(0, True)
    z_send(0, False)
    l1_send(st, l1, D1, 0)
    l1_send(st, l1, D1, 1)

    tri = (lax.broadcasted_iota(jnp.int32, (T, T), 0)
           >= lax.broadcasted_iota(jnp.int32, (T, T), 1))

    def q_phase(i):
        p = features(q_ref, i)
        pq[i] = p
        qb = p.astype(BF16)
        qf[i] = qb
        am = jnp.where(tri, dot_nt(qb, kf[i]), 0.0)
        rs[i] = jnp.sum(am, axis=-1, keepdims=True)
        amb = am.astype(BF16)
        ab[i] = amb
        nv[i] = dot_nn(amb, v_ref[:, head_cols(i)])

    atp = []
    ats = rcopy(at.at[pl.ds((1 - rep) * 2, 2)], atg.at[1, xl], ATS, sib)

    def attn_chunk(h):
        for i in (2 * h, 2 * h + 1):
            a = (nv[i] + dot_nn(qf[i], pr[i])) * rd[i]
            attn[i] = a
            at[i] = a.astype(BF16).T
        src = at.at[pl.ds(h * 2, 2)]
        c = rcopy(src, atg.at[(rep + h) % 2, xl], ATP + (rep + h) % 2, {"ctx": pair_ctx, "rep": h})
        c.start()
        atp.append(c)

        @pl.when(rep != h)
        def _():
            ats.start()

        @pl.when(rep == h)
        def _():
            atg[0, xl] = at[h * 2:h * 2 + 2]

    local[3].wait()
    q_phase(0)
    q_phase(1)
    a_got(0, 0)
    a_got(3, 0)
    a_got(0, 1)
    a_got(0, 3)
    b_recv(0, True)
    b_recv(0, False)
    q_phase(2)
    l1_turn(st, l1, tot, l2, D1, 1)
    b_recv(1, True)
    b_recv(1, False)
    a_got(0, 2)
    q_phase(3)

    each(earlier, lambda d: row_copy(zs, zr, ZB, d, 1).wait_recv())
    zsum = lax.fori_loop(1, ctx + 1, lambda d, a: a + zr[d], jnp.zeros((8, DH), F32))
    zpre[...] = zsum
    for i in range(HL):
        den = rs[i] + jnp.sum(qf[i].astype(F32) * get_row(zsum, i), axis=-1, keepdims=True)
        rd[i] = 1.0 / den

    a_got(1, 0)
    a_got(3, 1)
    l2_turn(l1, tot, l2, pf, pr, D1, 1)
    a_got(1, 3)
    b_recv(2, True)
    b_recv(2, False)
    l3_done(pf, pr, D1)
    attn_chunk(0)
    a_got(1, 2)
    a_got(1, 1)
    a_got(3, 3)
    b_recv(3, True)
    attn_chunk(1)
    local[5].wait()

    def go_part(mine):
        tok = xl if mine else 1 - xl

        def tile(m, _):
            rows = pl.ds(pl.multiple_of(m * 128, 128), 128)
            acc = dot_nt(ogg[0, 0, tok, rows, :], owg[0])
            for b in range(1, 8):
                acc += dot_nt(ogg[0, b, tok, rows, :], owg[b])
            if mine:
                gacc[rows, :] = acc
            else:
                gsend[rows, :] = acc.astype(BF16)
            return 0

        lax.fori_loop(0, 2, tile, 0)

    for c in bc:
        c.wait_recv()
    a_got(2, 1)
    a_got(2, 3)
    go_part(False)
    gx = rcopy(gsend, grecv, GX, pair)
    gx.start()

    a_got(3, 2)
    a_got(2, 0)
    a_got(2, 2)
    ats.wait_recv()
    for n in range(2):
        rcopy(atg.at[n, xl], atg.at[n, xl], ATP + n, pair).wait_recv()
    for c in ac.values():
        c.wait_recv()

    def w_block(b, ch):
        out = None
        for s in range(2):
            for t in range(2):
                d = dot_nn(atg[s, t, ch], ogg[s, b, t])
                out = d if out is None else out + d
        return out

    cp, cm = {}, {}

    def c_ready(s):
        for ch in range(2):
            if s < 4:
                wpre[0, ch] = w_block((z + 4 - s) % NZ, ch)
                if s < 3:
                    wpre[1, ch] = w_block((z + 5 + s) % NZ, ch)
            else:
                wpre[0, ch] = w_block(z, ch)

    def c_step(s, ch, up):
        sb, rb, cc = (cps, crp, cp) if up else (cms, crm, cm)
        if s == 0:
            val = w_block((z + 4) % NZ if up else (z + 5) % NZ, ch)
        else:
            val = wpre[0 if up else 1, ch]
            cc[s - 1, ch].wait_recv()
            val += rb[s - 1, ch].astype(F32)
        sb[s, ch] = val.astype(BF16)
        c = rcopy(sb.at[s, ch], rb.at[s, ch], (CP if up else CM) + 2 * s + ch, zp if up else zm)
        c.start()
        cc[s, ch] = c

    def c_round(s):
        for ch in range(2):
            c_step(s, ch, True)
            if s < 3:
                c_step(s, ch, False)

    c_round(0)
    go_part(True)
    c_ready(1)

    gx.wait_recv()

    def g_chunk(h):
        for i in (2 * h, 2 * h + 1):
            cols = head_cols(i)
            go = gacc[:, cols] + grecv[:, cols].astype(F32)
            r = rd[i]
            gb = (go * r).astype(BF16)
            gnb[i] = gb
            g = -jnp.sum(go * attn[i], axis=-1, keepdims=True) * r
            gd[i] = g
            qb = qf[i]
            st2[i] = dot_tn(qb, gb).astype(BF16)
            put_row(rs2, i, jnp.sum(qb.astype(F32) * g, axis=0, keepdims=True))
        l1_send(st2, l12, D2, h)

    g_chunk(0)
    g_chunk(1)
    each(earlier, lambda d: row_copy(rs2, rr2, RB, d, -1).start())

    def back(i, x_ref, w, out_ref):
        hi = w.astype(BF16)
        lo = (w - hi.astype(F32)).astype(BF16)
        t = dot_nn(hi, wc[i]) + dot_nn(lo, wc[i])
        u = t[:, 0:DH] + t[:, DH:2 * DH]
        xf = x_ref[:, head_cols(i)].astype(F32) * C
        out_ref[:, head_cols(i)] = (C * (u - xf * jnp.sum(w, axis=-1, keepdims=True))).astype(BF16)

    def dq_phase(i):
        gb, g, kb, qb = gnb[i], gd[i], kf[i], qf[i]
        bm = jnp.where(tri, dot_nt(gb, v_ref[:, head_cols(i)]) + g, 0.0).astype(BF16)
        dq = dot_nn(bm, kb) + dot_nt(gb, pr[i]) + g * get_row(zpre[...], i)
        back(i, q_ref, dq * pq[i], qg_ref)
        dk0[i] = dot_tn(bm, qb)
        dv0[i] = dot_tn(ab[i], gb)

    outs = []

    def out(src, dst):
        c = pltpu.make_async_copy(src, dst, lsem.at[6 + len(outs)])
        c.start()
        outs.append(c)

    c_round(1)
    c_ready(2)
    dq_phase(0)
    l1_turn(st2, l12, tot2, l22, D2, -1)
    c_round(2)
    c_ready(3)
    dq_phase(1)
    l2_turn(l12, tot2, l22, pf2, pr2, D2, -1)
    c_round(3)
    c_ready(4)
    dq_phase(2)
    dq_phase(3)
    out(qg_ref, qg_hbm)

    each(later, lambda d: row_copy(rs2, rr2, RB, d, -1).wait_recv())
    rsum = lax.fori_loop(1, later + 1, lambda d, a: a + rr2[d], jnp.zeros((8, DH), F32))

    ccs = []

    def c_last(ch):
        own = wpre[0, ch]
        cp[3, ch].wait_recv()
        cm[2, ch].wait_recv()
        rows = pl.ds(pl.multiple_of(rep * 256 + ch * DH, DH), DH)
        wg_ref[ch] = (own + crp[3, ch].astype(F32) + crm[2, ch].astype(F32)).astype(BF16)
        c = rcopy(wg_ref.at[ch], wg_hbm.at[rows], CC + ch, sib)
        c.start()
        ccs.append(c)
        out(wg_ref.at[ch], wg_hbm.at[rows])

    def dk_chunk(h):
        for i in (2 * h, 2 * h + 1):
            s = pr2[i]
            vb = v_ref[:, head_cols(i)]
            dk = dk0[i] + dot_nt(vb, s) + get_row(rsum, i)
            back(i, k_ref, dk * pk[i], kg_ref)
            vg_ref[:, head_cols(i)] = (dv0[i] + dot_nn(kf[i], s)).astype(BF16)
        cols = slice(h * 256, h * 256 + 256)
        out(kg_ref.at[:, cols], kg_hbm.at[:, cols])
        out(vg_ref.at[:, cols], vg_hbm.at[:, cols])

    l3_done(pf2, pr2, D2)
    dk_chunk(0)
    c_last(0)
    c_last(1)
    dk_chunk(1)

    for group in (ax, ayp, aym, ay2, ac, cp, cm, bzp, bzm):
        for c in group.values():
            c.wait_send()
    for c in bc + atp + [ats, gx]:
        c.wait_send()
    scan_sent(st, l1, tot, l2, pf, pr, D1, 1)
    scan_sent(st2, l12, tot2, l22, pf2, pr2, D2, -1)
    each(later, lambda d: row_copy(zs, zr, ZB, d, 1).wait_send())
    each(earlier, lambda d: row_copy(rs2, rr2, RB, d, -1).wait_send())
    for c in ccs + outs:
        c.wait()


def store(*refs):
    ins, outs, bufs, sem = refs[0:4], refs[4:8], refs[8:12], refs[12]
    load = [pltpu.make_async_copy(a, b, sem.at[i]) for i, (a, b) in enumerate(zip(ins, bufs))]
    save = [pltpu.make_async_copy(a, b, sem.at[4 + i]) for i, (a, b) in enumerate(zip(bufs, outs))]
    for c in load:
        c.start()
    for c, d in zip(load, save):
        c.wait()
        d.start()
    for d in save:
        d.wait()


def on_device(queries, key_vecs, values, out_grad, out_weight, sign_bits):
    flat = lambda a: a.reshape(T, HL * DH)
    hbm = pl.BlockSpec(memory_space=pltpu.HBM)
    state = pltpu.VMEM((HL, M, DH), BF16)
    total = pltpu.VMEM((M, DH), BF16)
    row = pltpu.VMEM((8, DH), F32)
    rows = pltpu.VMEM((NC, 8, DH), F32)
    heads = lambda n, dt: pltpu.VMEM((HL, T, n), dt)
    blocks = lambda n: pltpu.VMEM((n, 2, DH, 256), BF16)
    act = pltpu.VMEM((T, HL * DH), BF16)
    shapes = [jax.ShapeDtypeStruct((T, HL * DH), BF16)] * 3 + [jax.ShapeDtypeStruct((HL * DH, 256), BF16)]
    grads = pl.pallas_call(
        kernel,
        out_shape=shapes,
        in_specs=[hbm] * 6,
        out_specs=[hbm] * 4,
        scratch_shapes=[
            act, act, act, pltpu.VMEM((3, HL, M), jnp.int32),
            act, act, act, pltpu.VMEM((2, DH, 256), BF16),
            pltpu.VMEM((2, 8, 2, T, 256), BF16),
            pltpu.VMEM((NZ, 512, 256), BF16),
            pltpu.VMEM((T, 512), F32),
            act, act,
            state, state, state, total, state, state,
            state, state, state, total, state, state, pltpu.VMEM((M, DH), F32),
            row, rows, row, rows, row,
            heads(256, BF16),
            heads(M, F32), heads(M, F32), heads(M, BF16), heads(M, BF16),
            heads(T, BF16), heads(DH, F32), heads(1, F32), heads(1, F32),
            heads(DH, F32),
            pltpu.VMEM((HL, DH, T), BF16),
            pltpu.VMEM((2, 2, 2, DH, T), BF16),
            heads(DH, BF16), heads(1, F32), heads(M, F32), heads(DH, F32),
            pltpu.VMEM((2, 2, DH, 256), F32), blocks(4), blocks(3), blocks(4), blocks(3),
            pltpu.SemaphoreType.DMA((NSEM,)),
            pltpu.SemaphoreType.DMA((NSEM,)),
            pltpu.SemaphoreType.DMA((13,)),
        ],
        compiler_params=pltpu.CompilerParams(
            collective_id=0, has_side_effects=True, vmem_limit_bytes=62 * 1024 * 1024),
        cost_estimate=pl.CostEstimate(
            flops=5 * 10**9, bytes_accessed=4 * 10**6, transcendentals=5 * 10**5),
        name="performer_back",
    )(flat(queries), flat(key_vecs), flat(values), flat(out_grad), out_weight, sign_bits.transpose(1, 0, 2))
    qg, kg, vg, wg = pl.pallas_call(
        store,
        out_shape=shapes,
        in_specs=[hbm] * 4,
        out_specs=[hbm] * 4,
        scratch_shapes=[act, act, act, pltpu.VMEM((HL * DH, 256), BF16), pltpu.SemaphoreType.DMA((8,))],
        compiler_params=pltpu.CompilerParams(vmem_limit_bytes=62 * 1024 * 1024),
        name="store",
    )(*grads)
    shaped = lambda a: a.reshape(1, T, HL * DH)
    return shaped(qg), shaped(kg), shaped(vg), wg


def solution(mesh):
    tok = P("rep", "ctx", "head")
    return jax.shard_map(
        on_device, mesh=mesh,
        in_specs=(tok, tok, tok, tok, P("head", "ctx"), P("head", None, None)),
        out_specs=(tok, tok, tok, P("head", "ctx")),
        check_vma=False,
    )
```
